256 devices in a mesh: dp: 16 (over z, core), fsdp: 16 (over x, y).
Axes of the slice: x: 4, y: 4, z: 8, core: 2. Of those that a mesh axis runs over, the one named last changes fastest.
Arguments:
- activations: bfloat16 [131072, 4096], P(('dp', 'fsdp'))
- cotangent: bfloat16 [131072, 1024], P(('dp', 'fsdp'))
- value_weights: bfloat16 [4096, 1024], P('fsdp'), may hold values from -0.09375 to 0.09375
- sign_flips: int32 [4096, 1024], P('fsdp'), may hold values from -1 to 1, as said below
- level_count: int32 [], replicated, may hold values from 48 to 96
Outputs:
- input_grad: bfloat16 [131072, 4096], P(('dp', 'fsdp'))
- weight_grad: float32 [4096, 1024], P('fsdp')
The draws below stay inside these ranges and needn't reach their ends.
Inputs may be any that keep to these rules, and one draw needn't show every extreme that they name: `sign_flips`: each entry is -1 or 1.
All inputs are finite; a program needn't handle non-finite values. Where the reference program divides by a largest or mean magnitude, that divisor is 1e-20 or more.
Results may differ from the reference program's by a relative error of at most 0.0035.
Values may be sent and summed in bfloat16 or wider, within the bound.
No kernel may reach another device: no remote copies, remote signals or barrier semaphores. Data moves between devices by JAX's collectives and lax.ppermute only.
A program may use at most 128 MiB of HBM per device.

```python
import math
import jax
import jax.numpy as jnp
from jax import lax

D_IN = 4096
KVW = 1024
BLOCK = 4096
TOKENS = 131072
N_DP = 16


def draw_activations(key, part):
    key = jax.random.fold_in(key, 11)
    key_col, key_val = jax.random.split(key, 2)
    column_scale = jnp.exp(jax.random.uniform(key_col, (D_IN,), jnp.float32, math.log(0.3), math.log(3.0)))
    values = jax.random.normal(key_val, (TOKENS, D_IN), jnp.float32)
    return (values * column_scale[None, :]).astype(jnp.bfloat16)


def draw_cotangent(key, part):
    key = jax.random.fold_in(key, 23)
    key_col, key_val = jax.random.split(key, 2)
    column_scale = jnp.exp(jax.random.uniform(key_col, (KVW,), jnp.float32, math.log(0.3), math.log(3.0)))
    position = jnp.arange(TOKENS, dtype=jnp.float32) / TOKENS
    values = jax.random.normal(key_val, (TOKENS, KVW), jnp.float32)
    ramp_factor = 1.0 + 2.0 * position
    scaled = values * column_scale[None, :] * ramp_factor[:, None] / math.sqrt(TOKENS)
    return scaled.astype(jnp.bfloat16)


def draw_sign_flips(key, part):
    key = jax.random.fold_in(key, 37)
    return 2 * jax.random.randint(key, (D_IN, KVW), 0, 2, jnp.int32) - 1


def block_scale(rng, extent, pieces, least, high):
    level, own = 1.0, jax.random.fold_in(rng, 6)
    for dim, shards_of in pieces:
        draws = jnp.exp(jax.random.uniform(jax.random.fold_in(own, dim), (shards_of,), jnp.float32, least / len(pieces), high / len(pieces)))
        level = level * jnp.repeat(draws, extent[dim] // shards_of).reshape([-1 if axis == dim else 1 for axis in range(len(extent))])
    return level


def noise(own_key, dims, scale, bound, cuts=(), kind=jnp.bfloat16):
    entries = scale * jax.random.normal(own_key, dims, jnp.float32)
    if cuts:
        entries = entries * block_scale(own_key, dims, cuts, -0.22, 0.18)
    return jnp.clip(entries, -bound, bound).astype(kind)


def setup_inputs(seed: int = 0) -> dict:
    key_list = jax.random.split(jax.random.key(seed), 6)
    return {
        "activations": draw_activations(jax.random.fold_in(key_list[5], 71), 0),
        "cotangent": draw_cotangent(jax.random.fold_in(key_list[5], 71), 0),
        "value_weights": noise(key_list[2], (D_IN, KVW), D_IN ** -0.5, 0.09375, ((0, 16),)),
        "sign_flips": draw_sign_flips(jax.random.fold_in(key_list[5], 71), 0),
        "level_count": jax.random.randint(key_list[4], (), 48, 97).astype(jnp.int32),
    }


def hadamard(matrix_size):
    positions = jnp.arange(matrix_size, dtype=jnp.int32)
    common_bits = jnp.bitwise_and(positions[:, None], positions[None, :])
    parity = jnp.zeros((matrix_size, matrix_size), jnp.int32)
    for bit_pos in range(max(matrix_size.bit_length() - 1, 0)):
        parity = parity + jnp.bitwise_and(jnp.right_shift(common_bits, bit_pos), 1)
    return (1 - 2 * jnp.bitwise_and(parity, 1)).astype(jnp.float32)

def transform(values, block_size):
    outer_size = block_size // 128
    outer_matrix = hadamard(outer_size)
    inner_matrix = hadamard(128)
    shaped = values.reshape(-1, outer_size, 128)
    step_one = jnp.einsum('bij,jk->bik', shaped, inner_matrix, precision=lax.Precision.HIGHEST)
    step_two = jnp.einsum('li,bik->blk', outer_matrix, step_one, precision=lax.Precision.HIGHEST)
    return step_two.reshape(values.shape) / math.sqrt(block_size)

def reference(activations, cotangent, value_weights, sign_flips, level_count):
    per_group = TOKENS // N_DP
    signs_float = sign_flips.astype(jnp.float32)

    def per_group_work(group_id):
        group_start = (group_id * per_group).astype(jnp.int32)
        group_inputs = lax.dynamic_slice_in_dim(activations, group_start, per_group, 0)
        group_cotangent = lax.dynamic_slice_in_dim(cotangent, group_start, per_group, 0)
        group_dx = jnp.dot(group_cotangent, value_weights.T, preferred_element_type=jnp.float32).astype(jnp.bfloat16)
        group_partial = lax.dot_general(group_inputs, group_cotangent, (((0,), (0,)), ((), ())), preferred_element_type=jnp.float32)
        return (group_dx, transform(signs_float * group_partial, BLOCK))
    dx_parts, rotated = lax.map(per_group_work, jnp.arange(N_DP, dtype=jnp.int32))
    input_grad = dx_parts.reshape(TOKENS, D_IN)
    count_blocks = D_IN * KVW // BLOCK
    by_block = rotated.reshape(N_DP, count_blocks, BLOCK)
    block_peak = lax.optimization_barrier(jnp.max(jnp.abs(by_block), axis=(0, 2))) + 1e-06
    level_float = level_count.astype(jnp.float32)
    levels = jnp.floor(by_block * (level_float / block_peak)[None, :, None] + 0.5).astype(jnp.bfloat16)
    level_total = lax.optimization_barrier(jnp.sum(levels.astype(jnp.float32), axis=0))
    decoded = level_total * (block_peak / level_float)[:, None]
    weight_grad = signs_float * transform(decoded.reshape(D_IN, KVW), BLOCK)
    return (input_grad, weight_grad)
```

```python
import math

import jax
import jax.numpy as jnp
from jax import lax
from jax.sharding import Mesh, PartitionSpec as P

BLOCK = 4096


def hadamard(matrix_size):
    positions = jnp.arange(matrix_size, dtype=jnp.int32)
    common_bits = jnp.bitwise_and(positions[:, None], positions[None, :])
    parity = jnp.zeros((matrix_size, matrix_size), jnp.int32)
    for bit_pos in range(max(matrix_size.bit_length() - 1, 0)):
        parity = parity + jnp.bitwise_and(jnp.right_shift(common_bits, bit_pos), 1)
    return (1 - 2 * jnp.bitwise_and(parity, 1)).astype(jnp.float32)


def transform(values, block_size):
    outer_size = block_size // 128
    outer_matrix = hadamard(outer_size)
    inner_matrix = hadamard(128)
    shaped = values.reshape(-1, outer_size, 128)
    step_one = jnp.einsum("bij,jk->bik", shaped, inner_matrix, precision=lax.Precision.HIGHEST)
    step_two = jnp.einsum("li,bik->blk", outer_matrix, step_one, precision=lax.Precision.HIGHEST)
    return step_two.reshape(values.shape) / math.sqrt(block_size)


def shards(activations, cotangent, value_weights, sign_flips, level_count):
    rows_here = value_weights.shape[0]
    kv_width = value_weights.shape[1]
    dp = ("z", "core")
    fsdp = ("x", "y")
    input_grad = lax.dot_general(
        cotangent,
        lax.all_gather(value_weights, fsdp, axis=0, tiled=True),
        (((1,), (1,)), ((), ())),
        preferred_element_type=jnp.float32,
    ).astype(jnp.bfloat16)
    partial_sum = lax.psum_scatter(
        lax.dot_general(
            activations, cotangent, (((0,), (0,)), ((), ())), preferred_element_type=jnp.float32
        ),
        fsdp,
        scatter_dimension=0,
        tiled=True,
    )
    signs_float = sign_flips.astype(jnp.float32)
    rotated = transform(signs_float * partial_sum, BLOCK)
    groups = lax.all_to_all(rotated, dp, 0, 0, tiled=True)
    level_float = level_count.astype(jnp.float32)
    by_block = groups.reshape(16, rows_here // 16 * kv_width // BLOCK, BLOCK)
    block_peak = jnp.max(jnp.abs(by_block), axis=(0, 2)) + 1e-06
    levels = jnp.floor(by_block * (level_float / block_peak)[None, :, None] + 0.5)
    totals = jnp.sum(levels, axis=0)
    decoded = totals * (block_peak / level_float)[:, None]
    back = transform(decoded.reshape(rows_here // 16, kv_width), BLOCK)
    weight_grad = signs_float * lax.all_gather(back, dp, axis=0, tiled=True)
    return (input_grad, weight_grad)


def solution(mesh):
    torus = Mesh(mesh.devices.reshape(8, 2, 4, 4), ("z", "core", "x", "y"))
    rows = P(("z", "core", "x", "y"), None)
    part = P(("x", "y"), None)
    return jax.shard_map(
        shards,
        mesh=torus,
        in_specs=(rows, rows, part, part, P()),
        out_specs=(rows, part),
        check_vma=False,
    )
```

```python
import jax
import jax.numpy as jnp
import numpy as np
from jax import lax
from jax.experimental import pallas as pl
from jax.experimental.pallas import tpu as pltpu
from jax.sharding import Mesh, PartitionSpec as P

NZ, NC, NX, NY = 8, 2, 4, 4
AXES = ("z", "core", "x", "y")
KV = 1024
TOK = 512
F32, BF16, I16, I32 = jnp.float32, jnp.bfloat16, jnp.int16, jnp.int32
VMEM = 56 * 1024 * 1024


def hadamard(size):
    positions = np.arange(size)
    common = positions[:, None] & positions[None, :]
    parity = np.zeros((size, size), np.int64)
    for bit in range(16):
        parity += (common >> bit) & 1
    return (1 - 2 * (parity & 1)).astype(np.float32)


def power(e):
    return jnp.exp2(e * 0.125)


def step_of(top, low):
    return jnp.ceil(jnp.log2(jnp.maximum(top, low)) * 8.0)


def encode(v, ce):
    u = v if ce is None else v * power(-ce)
    e = step_of(jnp.max(jnp.abs(u), axis=1, keepdims=True), 1e-30) - 119.0
    q = jnp.floor(u * power(-e) + 0.5)
    return q.astype(I32).astype(I16), e


def to_float(q):
    return q.astype(I32).astype(F32)


def eye():
    return lax.broadcasted_iota(I32, (128, 128), 0) == lax.broadcasted_iota(I32, (128, 128), 1)


def to_lanes(col):
    return jnp.sum(jnp.where(eye(), col, 0.0), axis=0, keepdims=True)


def to_rows(row):
    return jnp.sum(jnp.where(eye(), row, 0.0), axis=1, keepdims=True)


def decode(q, row_e, ce_own, ce_oth):
    v = to_float(q) * power(to_rows(row_e))
    half = q.shape[0] // 2
    return v[:half] * power(ce_own), v[half:] * power(ce_oth)


def product(a, c):
    return lax.dot_general(a, c, (((0,), (0,)), ((), ())), preferred_element_type=F32)


def column_steps(c):
    top = jnp.max(jnp.abs(c.astype(F32)), axis=0, keepdims=True)
    return jnp.clip(step_of(top, 1e-30), -800.0, 800.0)


def far_kernel(idx, a_own, a_oth, c_own, c_oth, up, down, ce_ref, ex_up, ex_down):
    k = pl.program_id(0)

    @pl.when(k == 0)
    def _():
        ce_ref[...] = jnp.zeros_like(ce_ref)
        ce_ref[1:2, :] = column_steps(c_own[...])
        ce_ref[2:3, :] = column_steps(c_oth[...])
        ex_up[...] = ce_ref[...]
        ex_down[...] = ce_ref[...]

    rows = pl.ds(pl.multiple_of(k * 128, 128), 128)
    lanes = rows
    q0, e0 = encode(product(a_own[...], c_own[...]), ce_ref[1:2, :])
    q1, e1 = encode(product(a_oth[...], c_oth[...]), ce_ref[2:3, :])
    up[rows, :] = jnp.concatenate([q0[:64], q1[:64]], 0)
    down[rows, :] = jnp.concatenate([q0[64:], q1[64:]], 0)
    ex_up[0:1, lanes] = to_lanes(jnp.concatenate([e0[:64], e1[:64]], 0))
    ex_down[0:1, lanes] = to_lanes(jnp.concatenate([e0[64:], e1[64:]], 0))

    @pl.when(k == 3)
    def _():
        up[512:528, :] = ex_up[...].astype(I32).astype(I16)
        down[512:528, :] = ex_down[...].astype(I32).astype(I16)


def near_kernel(first, idx, a_own, a_oth, c_own, c_oth, ce, msg, keep, ex):
    k = pl.program_id(0)

    @pl.when(k == 0)
    def _():
        ex[...] = ce[...]

    rows = pl.ds(pl.multiple_of(k * 128, 128), 128)
    p0 = product(a_own[...], c_own[...])
    p1 = product(a_oth[...], c_oth[...])
    kept, sent = (slice(0, 64), slice(64, 128)) if first else (slice(64, 128), slice(0, 64))
    keep[...] = jnp.concatenate([p0[kept], p1[kept]], 0)
    q0, e0 = encode(p0[sent], ce[1:2, :])
    q1, e1 = encode(p1[sent], ce[2:3, :])
    msg[rows, :] = jnp.concatenate([q0, q1], 0)
    ex[0:1, rows] = to_lanes(jnp.concatenate([e0, e1], 0))

    @pl.when(k == 3)
    def _():
        msg[512:528, :] = ex[...].astype(I32).astype(I16)


def own_kernel(idx, a_own, a_oth, c_own, c_oth, keep):
    keep[0:128, :] = product(a_own[...], c_own[...])
    keep[128:256, :] = product(a_oth[...], c_oth[...])


def relay_kernel(keep, ce, q, q_ex, msg, ex):
    k = pl.program_id(0)
    rows = pl.ds(pl.multiple_of(k * 128, 128), 128)
    came = to_float(q_ex[...])

    @pl.when(k == 0)
    def _():
        ex[...] = jnp.maximum(ce[...], came)

    row_e = to_float(q_ex[:, rows])[0:1, :]
    d0, d1 = decode(q[...], row_e, came[1:2, :], came[2:3, :])
    q0, e0 = encode(keep[0:64, :] + d0, ex[1:2, :])
    q1, e1 = encode(keep[64:128, :] + d1, ex[2:3, :])
    msg[rows, :] = jnp.concatenate([q0, q1], 0)
    ex[0:1, rows] = to_lanes(jnp.concatenate([e0, e1], 0))

    @pl.when(k == 3)
    def _():
        msg[512:528, :] = ex[...].astype(I32).astype(I16)


def cross_kernel(keep, ce, ua, ua_ex, ub, ub_ex, da, da_ex, db, db_ex, own, n1, n2, n3, ex):
    k = pl.program_id(0)
    lanes = pl.ds(pl.multiple_of(k * 128, 128), 128)
    steps = [to_float(r[...]) for r in (ua_ex, ub_ex, da_ex, db_ex)]

    def get(q, q_ex, came):
        return decode(q[...], to_float(q_ex[:, lanes])[0:1, :], came[1:2, :], came[2:3, :])

    ua0, ua1 = get(ua, ua_ex, steps[0])
    ub0, ub1 = get(ub, ub_ex, steps[1])
    da0, da1 = get(da, da_ex, steps[2])
    db0, db1 = get(db, db_ex, steps[3])
    s0 = keep[0:128, :] + jnp.concatenate([ua0 + da0, ub0 + db0], 0)
    s1 = keep[128:256, :] + jnp.concatenate([ua1 + da1, ub1 + db1], 0)

    @pl.when(k == 0)
    def _():
        own[0:128, :] = s0
        own[128:256, :] = s1

    for number, msg in ((1, n1), (2, n2), (3, n3)):

        @pl.when(k == number)
        def _(msg=msg):
            ex[...] = jnp.maximum(jnp.maximum(ce[...], steps[0]), jnp.maximum(steps[1], jnp.maximum(steps[2], steps[3])))
            q0, e0 = encode(s0, ex[1:2, :])
            q1, e1 = encode(s1, ex[2:3, :])
            msg[0:128, :] = q0
            msg[128:256, :] = q1
            ex[0:1, 0:128] = to_lanes(e0)
            ex[0:1, 128:256] = to_lanes(e1)
            msg[256:272, :] = ex[...].astype(I32).astype(I16)


def split_dot(x, m):
    hi = x.astype(BF16)
    rest = x - hi.astype(F32)
    mid = rest.astype(BF16)
    lo = (rest - mid.astype(F32)).astype(BF16)
    dot = lambda a: jnp.dot(a, m, preferred_element_type=F32)
    return dot(hi) + (dot(mid) + dot(lo))


def split_dot_left(m, x):
    hi = x.astype(BF16)
    rest = x - hi.astype(F32)
    mid = rest.astype(BF16)
    lo = (rest - mid.astype(F32)).astype(BF16)
    dot = lambda a: jnp.dot(m, a, preferred_element_type=F32)
    return dot(hi) + (dot(mid) + dot(lo))


def rotate(v, inner, rows):
    tiles = [v[:, k * 128 : (k + 1) * 128] for k in range(8)]
    for bit in (1, 2, 4):
        tiles = [tiles[k ^ bit] - tiles[k] if k & bit else tiles[k] + tiles[k ^ bit] for k in range(8)]
    mixed = jnp.concatenate([split_dot(t, inner) for t in tiles], 1)
    return split_dot_left(rows, mixed) * (1.0 / 64.0)


def rotate_kernel(core, own, signs, n1, n2, n3, inner, rows, out):
    total = [own[0:128, :], own[128:256, :]]
    for msg in (n1, n2, n3):
        extra = to_float(msg[256:272, :])
        for g in (0, 1):
            e = to_rows(extra[0:1, g * 128 : (g + 1) * 128])
            total[g] += to_float(msg[g * 128 : (g + 1) * 128, :]) * power(e) * power(extra[1 + g : 2 + g, :])
    flips = signs[...].astype(F32)
    for g in (0, 1):
        q, e = encode(rotate(total[g] * flips, inner[...], rows[...]), None)
        wide = jnp.broadcast_to(e, (128, 128)).astype(I32).astype(I16)
        for z in range(NZ):
            out[z * 32 + g * 16 : z * 32 + g * 16 + 16, 0:KV] = q[z * 16 : z * 16 + 16]
            out[z * 32 + g * 16 : z * 32 + g * 16 + 16, KV : KV + 128] = wide[z * 16 : z * 16 + 16]


def levels_kernel(count, x, inner, rows, out):
    level = count[0].astype(F32)

    def group(g):
        q = x[g * 16 : g * 16 + 16, :]
        e = to_float(q[:, KV : KV + 128])[:, 0:1]
        return to_float(q[:, 0:KV]) * power(e)

    groups = [group(g) for g in range(NZ * NC)]
    top = jnp.abs(groups[0])
    for v in groups[1:]:
        top = jnp.maximum(top, jnp.abs(v))
    top = jnp.max(top, axis=1, keepdims=True)
    block = lax.shift_right_logical(lax.broadcasted_iota(I32, (16, 1), 0), 2)
    peak = jnp.zeros((16, 1), F32)
    for b in range(4):
        peak = jnp.where(block == b, jnp.max(jnp.where(block == b, top, 0.0), axis=0, keepdims=True), peak)
    peak = peak + 1e-06
    scale = level / peak
    total = jnp.floor(groups[0] * scale + 0.5)
    for v in groups[1:]:
        total = total + jnp.floor(v * scale + 0.5)
    q, e = encode(rotate(total * (peak / level), inner[...], rows[...]), None)
    out[:, 0:KV] = q
    out[:, KV : KV + 128] = jnp.broadcast_to(e, (16, 128)).astype(I32).astype(I16)


def finish_kernel(q, signs, out):
    for z in range(NZ):
        for c in range(NC):
            came = q[(z * NC + c) * 16 : (z * NC + c) * 16 + 16, :]
            rows = slice(c * 128 + z * 16, c * 128 + z * 16 + 16)
            e = to_float(came[:, KV : KV + 128])[:, 0:1]
            out[rows, :] = signs[rows, :].astype(F32) * (to_float(came[:, 0:KV]) * power(e))


def input_grad_kernel(core, c, w_own, w_oth, out):
    def part(w):
        return lax.dot_general(c[...], w[...], (((1,), (1,)), ((), ())), preferred_element_type=F32).astype(BF16)

    here = pl.multiple_of(core[0] * 128, 128)
    there = pl.multiple_of(128 - core[0] * 128, 128)
    out[:, pl.ds(here, 128)] = part(w_own)
    out[:, pl.ds(there, 128)] = part(w_oth)


def pick_kernel(core, a, out, sems):
    copies = []
    for k in range(NX * NY):
        start = pl.multiple_of(k * 256 + 128 - core[0] * 128, 128)
        copies.append(pltpu.make_async_copy(a.at[:, pl.ds(start, 128)], out.at[:, k * 128 : (k + 1) * 128], sems.at[k]))
    for copy in copies:
        copy.start()
    for copy in copies:
        copy.wait()


def tie_kernel(w, after, out):
    del w, after, out


def params():
    return pltpu.CompilerParams(vmem_limit_bytes=VMEM)


def cost(flops, moved):
    return pl.CostEstimate(flops=int(flops), bytes_accessed=int(moved), transcendentals=0)


def whole(shape):
    return pl.BlockSpec(shape, lambda *_: (0,) * len(shape))


def shift(s, first):
    pairs = []
    for z in range(NZ):
        for c in range(NC):
            for x in range(NX):
                for y in range(NY):
                    along_x = (c == 0) == first
                    tx, ty = ((x + s) % NX, y) if along_x else (x, (y + s) % NY)
                    pairs.append((((z * NC + c) * NX + x) * NY + y, ((z * NC + c) * NX + tx) * NY + ty))
    return pairs


def shards(activations, cotangent, value_weights, sign_flips, level_count):
    core = lax.axis_index("core").astype(I32)
    x, y = lax.axis_index("x").astype(I32), lax.axis_index("y").astype(I32)
    core1 = core.reshape(1)
    swap = lambda v: lax.ppermute(v, "core", [(0, 1), (1, 0)])
    send = lambda v, s, first: lax.ppermute(v, AXES, shift(s, first))
    sds = jax.ShapeDtypeStruct

    picked = pl.pallas_call(
        pick_kernel,
        out_shape=sds((TOK, 2048), BF16),
        grid_spec=pltpu.PrefetchScalarGridSpec(
            num_scalar_prefetch=1,
            grid=(1,),
            in_specs=[pl.BlockSpec(memory_space=pl.ANY)],
            out_specs=pl.BlockSpec(memory_space=pl.ANY),
            scratch_shapes=[pltpu.SemaphoreType.DMA((NX * NY,))],
        ),
        compiler_params=params(),
        cost_estimate=cost(0, 4 << 20),
        name="pick",
    )(core1, activations)
    a_oth = swap(picked)
    c_oth = swap(cotangent)

    half_w = lax.dynamic_slice_in_dim(value_weights, core * 128, 128, 0)
    w_own = lax.all_gather(half_w, ("x", "y"), axis=0, tiled=True)

    def indices(dp):
        ids = []
        for dq in range(4):
            tx = jnp.where(core == 0, (x + dp) % NX, (x + dq) % NX)
            ty = jnp.where(core == 0, (y + dq) % NY, (y + dp) % NY)
            ids.append(tx * NY + ty)
        return jnp.stack(ids + [core]).astype(I32)

    operands = [
        pl.BlockSpec((TOK, 128), lambda k, idx: (0, 2 * idx[k] + idx[4])),
        pl.BlockSpec((TOK, 128), lambda k, idx: (0, idx[k])),
        whole((TOK, KV)),
        whole((TOK, KV)),
    ]
    inputs = (activations, a_oth, cotangent, c_oth)
    message = sds((528, KV), I16)
    extra = pltpu.VMEM((16, KV), F32)
    mm = 2 * 1024 * 1024 * 512

    up1, down1, ce = pl.pallas_call(
        far_kernel,
        out_shape=(message, message, sds((16, KV), F32)),
        grid_spec=pltpu.PrefetchScalarGridSpec(
            num_scalar_prefetch=1,
            grid=(4,),
            in_specs=operands,
            out_specs=(whole((528, KV)), whole((528, KV)), whole((16, KV))),
            scratch_shapes=[extra, extra],
        ),
        compiler_params=params(),
        cost_estimate=cost(mm, 6 << 20),
        name="far",
    )(indices(2), *inputs)
    got_up1 = send(up1, 1, True)
    got_down1 = send(down1, -1, True)

    def near(dp, first):
        return pl.pallas_call(
            lambda *refs: near_kernel(first, *refs),
            out_shape=(message, sds((512, KV), F32)),
            grid_spec=pltpu.PrefetchScalarGridSpec(
                num_scalar_prefetch=1,
                grid=(4,),
                in_specs=operands + [whole((16, KV))],
                out_specs=(whole((528, KV)), pl.BlockSpec((128, KV), lambda k, idx: (k, 0))),
                scratch_shapes=[extra],
            ),
            compiler_params=params(),
            cost_estimate=cost(mm, 7 << 20),
            name="near",
        )(indices(dp), *inputs, ce)

    up2, keep_up = near(1, True)
    down2, keep_down = near(-1, False)
    got_up2 = send(up2, 1, True)
    got_down2 = send(down2, -1, True)

    keep = pl.pallas_call(
        own_kernel,
        out_shape=sds((1024, KV), F32),
        grid_spec=pltpu.PrefetchScalarGridSpec(
            num_scalar_prefetch=1,
            grid=(4,),
            in_specs=operands,
            out_specs=pl.BlockSpec((256, KV), lambda k, idx: (k, 0)),
        ),
        compiler_params=params(),
        cost_estimate=cost(mm, 8 << 20),
        name="own",
    )(indices(0), *inputs)

    codes = [pl.BlockSpec((128, KV), lambda k: (k, 0)), pl.BlockSpec((16, KV), lambda k: (32, 0))]

    def relay(kept, got):
        return pl.pallas_call(
            relay_kernel,
            out_shape=message,
            grid=(4,),
            in_specs=[pl.BlockSpec((128, KV), lambda k: (k, 0)), whole((16, KV))] + codes,
            out_specs=whole((528, KV)),
            scratch_shapes=[extra],
            compiler_params=params(),
            cost_estimate=cost(1 << 20, 4 << 20),
            name="relay",
        )(kept, ce, got, got)

    got_up3 = send(relay(keep_up, got_up1), 1, True)
    got_down3 = send(relay(keep_down, got_down1), -1, True)

    short = sds((272, KV), I16)
    own, n1, n2, n3 = pl.pallas_call(
        cross_kernel,
        out_shape=(sds((256, KV), F32), short, short, short),
        grid=(4,),
        in_specs=[pl.BlockSpec((256, KV), lambda k: (k, 0)), whole((16, KV))] + codes * 4,
        out_specs=(whole((256, KV)), whole((272, KV)), whole((272, KV)), whole((272, KV))),
        scratch_shapes=[extra],
        compiler_params=params(),
        cost_estimate=cost(1 << 20, 10 << 20),
        name="cross",
    )(keep, ce, got_up3, got_up3, got_up2, got_up2, got_down2, got_down2, got_down3, got_down3)
    g1 = send(n1, 1, False)
    g3 = send(n3, -1, False)
    g2 = send(n2, 2, False)

    w_own = pl.pallas_call(
        tie_kernel,
        out_shape=sds((2048, KV), BF16),
        in_specs=[pl.BlockSpec(memory_space=pl.ANY)] * 2,
        out_specs=pl.BlockSpec(memory_space=pl.ANY),
        input_output_aliases={0: 0},
        name="tie",
    )(w_own, n1)
    w_oth = swap(w_own)

    inner = jnp.asarray(hadamard(128), BF16)
    quad = hadamard(4)
    spun = pl.pallas_call(
        rotate_kernel,
        out_shape=sds((256, KV + 128), I16),
        grid_spec=pltpu.PrefetchScalarGridSpec(
            num_scalar_prefetch=1,
            grid=(1,),
            in_specs=[
                whole((256, KV)),
                pl.BlockSpec((128, KV), lambda k, c: (c[0], 0)),
                whole((272, KV)),
                whole((272, KV)),
                whole((272, KV)),
                whole((128, 128)),
                whole((128, 128)),
            ],
            out_specs=whole((256, KV + 128)),
        ),
        compiler_params=params(),
        cost_estimate=cost(1 << 28, 4 << 20),
        name="rotate",
    )(core1, own, sign_flips, g1, g2, g3, inner, jnp.asarray(np.kron(np.eye(32), quad), BF16))
    groups = lax.all_to_all(spun, "z", 0, 0, tiled=True)

    back = pl.pallas_call(
        levels_kernel,
        out_shape=sds((16, KV + 128), I16),
        in_specs=[pl.BlockSpec(memory_space=pltpu.SMEM)] + [pl.BlockSpec(memory_space=pltpu.VMEM)] * 3,
        out_specs=pl.BlockSpec(memory_space=pltpu.VMEM),
        compiler_params=params(),
        cost_estimate=cost(1 << 26, 1 << 20),
        name="levels",
    )(level_count.reshape(1), groups, inner, jnp.asarray(np.kron(np.eye(4), quad), BF16))
    gathered = lax.all_gather(back, ("z", "core"), axis=0, tiled=True)
    weight_grad = pl.pallas_call(
        finish_kernel,
        out_shape=sds((256, KV), F32),
        in_specs=[pl.BlockSpec(memory_space=pltpu.VMEM)] * 2,
        out_specs=pl.BlockSpec(memory_space=pltpu.VMEM),
        compiler_params=params(),
        cost_estimate=cost(1 << 20, 3 << 20),
        name="finish",
    )(gathered, sign_flips)

    input_grad = pl.pallas_call(
        input_grad_kernel,
        out_shape=sds((TOK, 4096), BF16),
        grid_spec=pltpu.PrefetchScalarGridSpec(
            num_scalar_prefetch=1,
            grid=(16,),
            in_specs=[
                whole((TOK, KV)),
                pl.BlockSpec((128, KV), lambda k, c: (k, 0)),
                pl.BlockSpec((128, KV), lambda k, c: (k, 0)),
            ],
            out_specs=pl.BlockSpec((TOK, 256), lambda k, c: (0, k)),
        ),
        compiler_params=params(),
        cost_estimate=cost(4 * mm, 13 << 20),
        name="input_grad",
    )(core1, cotangent, w_own, w_oth)
    return (input_grad, weight_grad)


def solution(mesh):
    torus = Mesh(mesh.devices.reshape(NZ, NC, NX, NY), AXES)
    rows = P(AXES, None)
    part = P(("x", "y"), None)
    return jax.shard_map(
        shards,
        mesh=torus,
        in_specs=(rows, rows, part, part, P()),
        out_specs=(rows, part),
        check_vma=False,
    )
```

```python
import jax
import jax.numpy as jnp
import numpy as np
from jax import lax
from jax.experimental import pallas as pl
from jax.experimental.pallas import tpu as pltpu
from jax.sharding import Mesh, PartitionSpec as P

NZ, NC, NX, NY = 8, 2, 4, 4
AXES = ("z", "core", "x", "y")
KV = 1024
TOK = 512
F32, BF16, I16, I32 = jnp.float32, jnp.bfloat16, jnp.int16, jnp.int32
VMEM = 56 * 1024 * 1024
SMALL = 24 * 1024 * 1024


def hadamard(size):
    positions = np.arange(size)
    common = positions[:, None] & positions[None, :]
    parity = np.zeros((size, size), np.int64)
    for bit in range(16):
        parity += (common >> bit) & 1
    return (1 - 2 * (parity & 1)).astype(np.float32)


def power(e):
    return jnp.exp2(e * 0.125)


def step_of(top, low):
    return jnp.ceil(jnp.log2(jnp.maximum(top, low)) * 8.0)


def encode(v, ce):
    u = v if ce is None else v * power(-ce)
    e = step_of(jnp.max(jnp.abs(u), axis=1, keepdims=True), 1e-30) - 119.0
    q = jnp.floor(u * power(-e) + 0.5)
    return q.astype(I32).astype(I16), e


def to_float(q):
    return q.astype(I32).astype(F32)


def eye():
    return lax.broadcasted_iota(I32, (128, 128), 0) == lax.broadcasted_iota(I32, (128, 128), 1)


def to_lanes(col):
    return jnp.sum(jnp.where(eye(), col, 0.0), axis=0, keepdims=True)


def to_rows(row):
    return jnp.sum(jnp.where(eye(), row, 0.0), axis=1, keepdims=True)


def write(msg, v, ce):
    count = v.shape[0]
    q, e = encode(v, ce)
    msg[0:count, :] = q
    parts = [to_lanes(e[k : k + 128]) for k in range(0, count, 128)]
    line = jnp.concatenate(parts + [jnp.zeros((1, KV - count), F32)], 1)
    row = lax.broadcasted_iota(I32, (16, KV), 0)
    extra = jnp.where(row == 0, line, jnp.where(row == 1, ce, 0.0))
    msg[count : count + 16, :] = extra.astype(I32).astype(I16)


def steps_in(msg):
    count = msg.shape[0] - 16
    return to_float(msg[count : count + 16, :])


def read(msg):
    count = msg.shape[0] - 16
    extra = steps_in(msg)
    e = jnp.concatenate([to_rows(extra[0:1, k : k + 128]) for k in range(0, count, 128)], 0)
    return to_float(msg[0:count, :]) * power(e) * power(extra[1:2, :])


def product(tiles, c):
    a = jnp.concatenate([t[...] for t in tiles], 1)
    return lax.dot_general(a, c[...], (((0,), (0,)), ((), ())), preferred_element_type=F32)


def column_steps(c):
    top = jnp.max(jnp.abs(c.astype(F32)), axis=0, keepdims=True)
    return jnp.clip(step_of(top, 1e-30), -800.0, 800.0)


def half(v, number):
    return jnp.concatenate([v[k + 64 * number : k + 64 * number + 64] for k in range(0, v.shape[0], 128)], 0)


def far_kernel(idx, t0, t1, t2, t3, c, up_x, down_x, up_y, down_y, ce):
    ce[...] = jnp.broadcast_to(column_steps(c[...]), (8, KV))
    p = product((t0, t1, t2, t3), c)
    for axis, (up, down) in enumerate(((up_x, down_x), (up_y, down_y))):

        @pl.when(pl.program_id(0) == axis)
        def _(up=up, down=down):
            write(up, half(p, 0), ce[0:1, :])
            write(down, half(p, 1), ce[0:1, :])


def near_kernel(idx, t0, t1, t2, t3, c, ce, up_x, down_x, up_y, down_y, keep):
    p = product((t0, t1, t2, t3), c)
    for step, msg in enumerate((up_x, down_x, up_y, down_y)):

        @pl.when(pl.program_id(0) == step)
        def _(step=step, msg=msg):
            kept = step % 2
            keep[...] = half(p, kept)
            write(msg, half(p, 1 - kept), ce[0:1, :])


def own_kernel(idx, t0, t1, t2, t3, c, keep):
    keep[...] = product((t0, t1, t2, t3), c)


def relay_kernel(keep, ce, *refs):
    for step in range(4):

        @pl.when(pl.program_id(0) == step)
        def _(got=refs[step], msg=refs[4 + step]):
            write(msg, keep[...] + read(got), jnp.maximum(ce[0:1, :], steps_in(got)[1:2, :]))


def cross_kernel(keep, ce, *refs):
    for axis in range(2):

        @pl.when(pl.program_id(0) == axis)
        def _(got=refs[4 * axis : 4 * axis + 4], out=refs[8 + 4 * axis : 12 + 4 * axis]):
            up2, down2, up3, down3 = got
            ce_all = ce[0:1, :]
            for msg in got:
                ce_all = jnp.maximum(ce_all, steps_in(msg)[1:2, :])
            first, last = read(up3) + read(down2), read(up2) + read(down3)
            for t in range(4):
                rows = slice(t * 64, t * 64 + 64)
                total = keep[t * 128 : t * 128 + 128, :] + jnp.concatenate([first[rows], last[rows]], 0)
                if t == 0:
                    out[0][...] = total
                else:
                    write(out[t], total, ce_all)


def split_dot(x, m):
    hi = x.astype(BF16)
    rest = x - hi.astype(F32)
    mid = rest.astype(BF16)
    lo = (rest - mid.astype(F32)).astype(BF16)
    dot = lambda a: jnp.dot(a, m, preferred_element_type=F32)
    return dot(hi) + (dot(mid) + dot(lo))


def split_dot_left(m, x):
    hi = x.astype(BF16)
    rest = x - hi.astype(F32)
    mid = rest.astype(BF16)
    lo = (rest - mid.astype(F32)).astype(BF16)
    dot = lambda a: jnp.dot(m, a, preferred_element_type=F32)
    return dot(hi) + (dot(mid) + dot(lo))


def rotate(v, inner, rows):
    tiles = [v[:, k * 128 : (k + 1) * 128] for k in range(8)]
    for bit in (1, 2, 4):
        tiles = [tiles[k ^ bit] - tiles[k] if k & bit else tiles[k] + tiles[k ^ bit] for k in range(8)]
    mixed = jnp.concatenate([split_dot(t, inner) for t in tiles], 1)
    return split_dot_left(rows, mixed) * (1.0 / 64.0)


def rotate_kernel(own_x, own_y, x1, x2, x3, y1, y2, y3, signs, inner, rows, out):
    for k, (own, msgs) in enumerate(((own_x, (x1, x2, x3)), (own_y, (y1, y2, y3)))):
        here = slice(k * 128, k * 128 + 128)
        total = own[...]
        for msg in msgs:
            total = total + read(msg)
        q, e = encode(rotate(total * signs[here, :].astype(F32), inner[...], rows[...]), None)
        out[here, 0:KV] = q
        out[here, KV : KV + 128] = jnp.broadcast_to(e, (128, 128)).astype(I32).astype(I16)


def levels_kernel(count, x, inner, rows, out):
    level = count[0].astype(F32)

    def group(g):
        q = x[g * 16 : g * 16 + 16, :]
        e = to_float(q[:, KV : KV + 128])[:, 0:1]
        return to_float(q[:, 0:KV]) * power(e)

    groups = [group(g) for g in range(NZ * NC)]
    top = jnp.abs(groups[0])
    for v in groups[1:]:
        top = jnp.maximum(top, jnp.abs(v))
    top = jnp.max(top, axis=1, keepdims=True)
    block = lax.shift_right_logical(lax.broadcasted_iota(I32, (16, 1), 0), 2)
    peak = jnp.zeros((16, 1), F32)
    for b in range(4):
        peak = jnp.where(block == b, jnp.max(jnp.where(block == b, top, 0.0), axis=0, keepdims=True), peak)
    peak = peak + 1e-06
    scale = level / peak
    total = jnp.floor(groups[0] * scale + 0.5)
    for v in groups[1:]:
        total = total + jnp.floor(v * scale + 0.5)
    q, e = encode(rotate(total * (peak / level), inner[...], rows[...]), None)
    out[:, 0:KV] = q
    out[:, KV : KV + 128] = jnp.broadcast_to(e, (16, 128)).astype(I32).astype(I16)


def finish_kernel(q, signs, out):
    e = to_float(q[:, KV : KV + 128])[:, 0:1]
    out[...] = signs[...].astype(F32) * (to_float(q[:, 0:KV]) * power(e))


def input_grad_kernel(core, c, w_own, w_oth, out, w):
    for k in range(4):
        rows = slice(k * 128, k * 128 + 128)
        w[pl.ds(pl.multiple_of(k * 256 + core[0] * 128, 128), 128), :] = w_own[rows, :]
        w[pl.ds(pl.multiple_of(k * 256 + 128 - core[0] * 128, 128), 128), :] = w_oth[rows, :]
    out[...] = lax.dot_general(c[...], w[...], (((1,), (1,)), ((), ())), preferred_element_type=F32).astype(BF16)


def tie_kernel(w, after, out):
    del w, after, out


def half_kernel(core, w, after, out):
    out[...] = w[...]


def params(limit=VMEM):
    return pltpu.CompilerParams(vmem_limit_bytes=limit)


def cost(flops, moved):
    return pl.CostEstimate(flops=int(flops), bytes_accessed=int(moved), transcendentals=0)


def whole(shape):
    return pl.BlockSpec(shape, lambda *_: (0,) * len(shape))


def shift(size, s):
    return [(k, (k + s) % size) for k in range(size)]


def shards(activations, cotangent, value_weights, sign_flips, level_count):
    core = lax.axis_index("core").astype(I32)
    x, y = lax.axis_index("x").astype(I32), lax.axis_index("y").astype(I32)
    sds = jax.ShapeDtypeStruct
    anywhere = pl.BlockSpec(memory_space=pl.ANY)
    in_vmem = pl.BlockSpec(memory_space=pltpu.VMEM)

    def send(v, axis, s):
        return lax.ppermute(v, "xy"[axis], shift((NX, NY)[axis], s))

    ids = []
    for axis in range(2):
        for dp in range(4):
            for dq in range(4):
                tx = (x + (dq if axis else dp)) % NX
                ty = (y + (dp if axis else dq)) % NY
                ids.append(2 * (tx * NY + ty) + axis)
    idx = jnp.stack(ids).astype(I32)

    def operands(where):
        tiles = [pl.BlockSpec((TOK, 128), lambda k, ids, t=t: (0, ids[where(k) + t])) for t in range(4)]
        return tiles + [whole((TOK, KV))]

    inputs = (activations,) * 4 + (cotangent,)
    message = pltpu.HBM((272, KV), I16)
    mm = 2 * 1024 * 1024 * 512

    up1x, down1x, up1y, down1y, ce = pl.pallas_call(
        far_kernel,
        out_shape=(message,) * 4 + (sds((8, KV), F32),),
        grid_spec=pltpu.PrefetchScalarGridSpec(
            num_scalar_prefetch=1,
            grid=(2,),
            in_specs=operands(lambda k: 16 * k + 8),
            out_specs=(whole((272, KV)),) * 4 + (whole((8, KV)),),
        ),
        compiler_params=params(),
        cost_estimate=cost(mm, 6 << 20),
        name="far",
    )(idx, *inputs)
    got1 = [send(up1x, 0, 1), send(down1x, 0, -1), send(up1y, 1, 1), send(down1y, 1, -1)]

    up2x, down2x, up2y, down2y, keep_near = pl.pallas_call(
        near_kernel,
        out_shape=(message,) * 4 + (sds((1024, KV), F32),),
        grid_spec=pltpu.PrefetchScalarGridSpec(
            num_scalar_prefetch=1,
            grid=(4,),
            in_specs=operands(lambda k: 16 * (k // 2) + 4 + 8 * (k % 2)) + [whole((8, KV))],
            out_specs=(whole((272, KV)),) * 4 + (pl.BlockSpec((256, KV), lambda k, ids: (k, 0)),),
        ),
        compiler_params=params(SMALL),
        cost_estimate=cost(2 * mm, 11 << 20),
        name="near",
    )(idx, *inputs, ce)
    got2 = [send(up2x, 0, 1), send(down2x, 0, -1), send(up2y, 1, 1), send(down2y, 1, -1)]

    keep = pl.pallas_call(
        own_kernel,
        out_shape=sds((1024, KV), F32),
        grid_spec=pltpu.PrefetchScalarGridSpec(
            num_scalar_prefetch=1,
            grid=(2,),
            in_specs=operands(lambda k: 16 * k),
            out_specs=pl.BlockSpec((512, KV), lambda k, ids: (k, 0)),
        ),
        compiler_params=params(SMALL),
        cost_estimate=cost(mm, 8 << 20),
        name="own",
    )(idx, *inputs)

    up3x, down3x, up3y, down3y = pl.pallas_call(
        relay_kernel,
        out_shape=(message,) * 4,
        grid=(4,),
        in_specs=[pl.BlockSpec((256, KV), lambda k: (k, 0)), whole((8, KV))] + [whole((272, KV))] * 4,
        out_specs=(whole((272, KV)),) * 4,
        compiler_params=params(SMALL),
        cost_estimate=cost(1 << 20, 8 << 20),
        name="relay",
    )(keep_near, ce, *got1)
    got3 = [send(up3x, 0, 1), send(down3x, 0, -1), send(up3y, 1, 1), send(down3y, 1, -1)]

    parts = pl.pallas_call(
        cross_kernel,
        out_shape=((pltpu.HBM((128, KV), F32),) + (pltpu.HBM((144, KV), I16),) * 3) * 2,
        grid=(2,),
        in_specs=[pl.BlockSpec((512, KV), lambda k: (k, 0)), whole((8, KV))] + [whole((272, KV))] * 8,
        out_specs=((whole((128, KV)),) + (whole((144, KV)),) * 3) * 2,
        compiler_params=params(SMALL),
        cost_estimate=cost(1 << 20, 12 << 20),
        name="cross",
    )(keep, ce, got2[0], got2[1], got3[0], got3[1], got2[2], got2[3], got3[2], got3[3])
    own_x, x1, x2, x3, own_y, y1, y2, y3 = parts
    last = [send(x1, 1, 1), send(x2, 1, 2), send(x3, 1, -1), send(y1, 0, 1), send(y2, 0, 2), send(y3, 0, -1)]

    half_w = pl.pallas_call(
        half_kernel,
        out_shape=pltpu.HBM((128, KV), BF16),
        grid_spec=pltpu.PrefetchScalarGridSpec(
            num_scalar_prefetch=1,
            grid=(1,),
            in_specs=[pl.BlockSpec((128, KV), lambda k, c: (c[0], 0)), anywhere],
            out_specs=whole((128, KV)),
        ),
        compiler_params=params(SMALL),
        name="half",
    )(core.reshape(1), value_weights, keep)
    w_own = lax.all_gather(half_w, ("x", "y"), axis=0, tiled=True)

    inner = jnp.asarray(hadamard(128), BF16)
    quad = hadamard(4)
    spun = pl.pallas_call(
        rotate_kernel,
        out_shape=sds((256, KV + 128), I16),
        in_specs=[in_vmem] * 11,
        out_specs=in_vmem,
        compiler_params=params(SMALL),
        cost_estimate=cost(1 << 28, 4 << 20),
        name="rotate",
    )(own_x, own_y, *last, sign_flips, inner, jnp.asarray(np.kron(np.eye(32), quad), BF16))
    groups = lax.all_to_all(spun, ("z", "core"), 0, 0, tiled=True)

    back = pl.pallas_call(
        levels_kernel,
        out_shape=sds((16, KV + 128), I16),
        in_specs=[pl.BlockSpec(memory_space=pltpu.SMEM)] + [in_vmem] * 3,
        out_specs=in_vmem,
        compiler_params=params(SMALL),
        cost_estimate=cost(1 << 26, 1 << 20),
        name="levels",
    )(level_count.reshape(1), groups, inner, jnp.asarray(np.kron(np.eye(4), quad), BF16))
    w_own = pl.pallas_call(
        tie_kernel,
        out_shape=sds((2048, KV), BF16),
        in_specs=[anywhere] * 2,
        out_specs=anywhere,
        input_output_aliases={0: 0},
        name="tie",
    )(w_own, back)
    w_oth = lax.ppermute(w_own, "core", shift(NC, 1))
    gathered = lax.all_gather(back, ("z", "core"), axis=0, tiled=True)
    weight_grad = pl.pallas_call(
        finish_kernel,
        out_shape=sds((256, KV), F32),
        in_specs=[in_vmem] * 2,
        out_specs=in_vmem,
        compiler_params=params(SMALL),
        cost_estimate=cost(1 << 20, 3 << 20),
        name="finish",
    )(gathered, sign_flips)
    input_grad = pl.pallas_call(
        input_grad_kernel,
        out_shape=pltpu.HBM((TOK, 4096), BF16),
        grid_spec=pltpu.PrefetchScalarGridSpec(
            num_scalar_prefetch=1,
            grid=(4,),
            in_specs=[
                whole((TOK, KV)),
                pl.BlockSpec((512, KV), lambda k, c: (k, 0)),
                pl.BlockSpec((512, KV), lambda k, c: (k, 0)),
            ],
            out_specs=pl.BlockSpec((TOK, 1024), lambda k, c: (0, k)),
            scratch_shapes=[pltpu.VMEM((1024, KV), BF16)],
        ),
        compiler_params=params(SMALL),
        cost_estimate=cost(4 * mm, 13 << 20),
        name="input_grad",
    )(core.reshape(1), cotangent, w_own, w_oth)

    return (input_grad, weight_grad)


def solution(mesh):
    torus = Mesh(mesh.devices.reshape(NZ, NC, NX, NY), AXES)
    rows = P(AXES, None)
    part = P(("x", "y"), None)
    return jax.shard_map(
        shards,
        mesh=torus,
        in_specs=(rows, rows, part, part, P()),
        out_specs=(rows, part),
        check_vma=False,
    )
```

```python
import jax
import jax.numpy as jnp
import numpy as np
from jax import lax
from jax.experimental import pallas as pl
from jax.experimental.pallas import tpu as pltpu
from jax.sharding import Mesh, PartitionSpec as P

NZ, NC, NX, NY = 8, 2, 4, 4
AXES = ("z", "core", "x", "y")
KV = 1024
TOK = 512
F32, BF16, I16, I32 = jnp.float32, jnp.bfloat16, jnp.int16, jnp.int32
VMEM = 56 * 1024 * 1024
SMALL = 24 * 1024 * 1024


def hadamard(size):
    positions = np.arange(size)
    common = positions[:, None] & positions[None, :]
    parity = np.zeros((size, size), np.int64)
    for bit in range(16):
        parity += (common >> bit) & 1
    return (1 - 2 * (parity & 1)).astype(np.float32)


def power(e):
    return jnp.exp2(e * 0.125)


def step_of(top, low):
    return jnp.ceil(jnp.log2(jnp.maximum(top, low)) * 8.0)


def encode(v, ce):
    u = v if ce is None else v * power(-ce)
    e = step_of(jnp.max(jnp.abs(u), axis=1, keepdims=True), 1e-30) - 119.0
    q = jnp.floor(u * power(-e) + 0.5)
    return q.astype(I32).astype(I16), e


def to_float(q):
    return q.astype(I32).astype(F32)


def eye():
    return lax.broadcasted_iota(I32, (128, 128), 0) == lax.broadcasted_iota(I32, (128, 128), 1)


def to_lanes(col):
    return jnp.sum(jnp.where(eye(), col, 0.0), axis=0, keepdims=True)


def to_rows(row):
    return jnp.sum(jnp.where(eye(), row, 0.0), axis=1, keepdims=True)


def write(msg, v, ce):
    count = v.shape[0]
    q, e = encode(v, ce)
    msg[0:count, :] = q
    parts = [to_lanes(e[k : k + 128]) for k in range(0, count, 128)]
    line = jnp.concatenate(parts + [jnp.zeros((1, KV - count), F32)], 1)
    row = lax.broadcasted_iota(I32, (16, KV), 0)
    extra = jnp.where(row == 0, line, jnp.where(row == 1, ce, 0.0))
    msg[count : count + 16, :] = extra.astype(I32).astype(I16)


def steps_in(msg):
    count = msg.shape[0] - 16
    return to_float(msg[count : count + 16, :])


def read(msg):
    count = msg.shape[0] - 16
    extra = steps_in(msg)
    e = jnp.concatenate([to_rows(extra[0:1, k : k + 128]) for k in range(0, count, 128)], 0)
    return to_float(msg[0:count, :]) * power(e) * power(extra[1:2, :])


def product(tiles, c):
    a = jnp.concatenate([t[...] for t in tiles], 1)
    return lax.dot_general(a, c[...], (((0,), (0,)), ((), ())), preferred_element_type=F32)


def column_steps(c):
    top = jnp.max(jnp.abs(c.astype(F32)), axis=0, keepdims=True)
    return jnp.clip(step_of(top, 1e-30), -800.0, 800.0)


def half(v, number):
    return jnp.concatenate([v[k + 64 * number : k + 64 * number + 64] for k in range(0, v.shape[0], 128)], 0)


def far_kernel(idx, t0, t1, t2, t3, c, up_x, down_x, up_y, down_y, ce):
    ce[...] = jnp.broadcast_to(column_steps(c[...]), (8, KV))
    p = product((t0, t1, t2, t3), c)
    for axis, (up, down) in enumerate(((up_x, down_x), (up_y, down_y))):

        @pl.when(pl.program_id(0) == axis)
        def _(up=up, down=down):
            write(up, half(p, 0), ce[0:1, :])
            write(down, half(p, 1), ce[0:1, :])


def near_kernel(idx, t0, t1, t2, t3, c, ce, up_x, down_x, up_y, down_y, keep):
    p = product((t0, t1, t2, t3), c)
    for step, msg in enumerate((up_x, down_x, up_y, down_y)):

        @pl.when(pl.program_id(0) == step)
        def _(step=step, msg=msg):
            kept = step % 2
            keep[...] = half(p, kept)
            write(msg, half(p, 1 - kept), ce[0:1, :])


def own_kernel(idx, t0, t1, t2, t3, c, keep):
    keep[...] = product((t0, t1, t2, t3), c)


def relay_kernel(keep, ce, *refs):
    for step in range(4):

        @pl.when(pl.program_id(0) == step)
        def _(got=refs[step], msg=refs[4 + step]):
            write(msg, keep[...] + read(got), jnp.maximum(ce[0:1, :], steps_in(got)[1:2, :]))


def cross_kernel(keep, ce, *refs):
    for axis in range(2):

        @pl.when(pl.program_id(0) == axis)
        def _(got=refs[4 * axis : 4 * axis + 4], out=refs[8 + 4 * axis : 12 + 4 * axis]):
            up2, down2, up3, down3 = got
            ce_all = ce[0:1, :]
            for msg in got:
                ce_all = jnp.maximum(ce_all, steps_in(msg)[1:2, :])
            first, last = read(up3) + read(down2), read(up2) + read(down3)
            for t in range(4):
                rows = slice(t * 64, t * 64 + 64)
                total = keep[t * 128 : t * 128 + 128, :] + jnp.concatenate([first[rows], last[rows]], 0)
                if t == 0:
                    out[0][...] = total
                else:
                    write(out[t], total, ce_all)


def split_dot(x, m):
    hi = x.astype(BF16)
    rest = x - hi.astype(F32)
    mid = rest.astype(BF16)
    lo = (rest - mid.astype(F32)).astype(BF16)
    dot = lambda a: jnp.dot(a, m, preferred_element_type=F32)
    return dot(hi) + (dot(mid) + dot(lo))


def split_dot_left(m, x):
    hi = x.astype(BF16)
    rest = x - hi.astype(F32)
    mid = rest.astype(BF16)
    lo = (rest - mid.astype(F32)).astype(BF16)
    dot = lambda a: jnp.dot(m, a, preferred_element_type=F32)
    return dot(hi) + (dot(mid) + dot(lo))


def rotate(v, inner, rows):
    tiles = [v[:, k * 128 : (k + 1) * 128] for k in range(8)]
    for bit in (1, 2, 4):
        tiles = [tiles[k ^ bit] - tiles[k] if k & bit else tiles[k] + tiles[k ^ bit] for k in range(8)]
    mixed = jnp.concatenate([split_dot(t, inner) for t in tiles], 1)
    return split_dot_left(rows, mixed) * (1.0 / 64.0)


def rotate_kernel(own_x, own_y, x1, x2, x3, y1, y2, y3, signs, inner, rows, out):
    for k, (own, msgs) in enumerate(((own_x, (x1, x2, x3)), (own_y, (y1, y2, y3)))):
        here = slice(k * 128, k * 128 + 128)
        total = own[...]
        for msg in msgs:
            total = total + read(msg)
        q, e = encode(rotate(total * signs[here, :].astype(F32), inner[...], rows[...]), None)
        out[here, 0:KV] = q
        out[here, KV : KV + 128] = jnp.broadcast_to(e, (128, 128)).astype(I32).astype(I16)


def levels_kernel(count, x, inner, rows, after, out):
    level = count[0].astype(F32)

    def group(g):
        q = x[g * 16 : g * 16 + 16, :]
        e = to_float(q[:, KV : KV + 128])[:, 0:1]
        return to_float(q[:, 0:KV]) * power(e)

    groups = [group(g) for g in range(NZ * NC)]
    top = jnp.abs(groups[0])
    for v in groups[1:]:
        top = jnp.maximum(top, jnp.abs(v))
    top = jnp.max(top, axis=1, keepdims=True)
    block = lax.shift_right_logical(lax.broadcasted_iota(I32, (16, 1), 0), 2)
    peak = jnp.zeros((16, 1), F32)
    for b in range(4):
        peak = jnp.where(block == b, jnp.max(jnp.where(block == b, top, 0.0), axis=0, keepdims=True), peak)
    peak = peak + 1e-06
    scale = level / peak
    total = jnp.floor(groups[0] * scale + 0.5)
    for v in groups[1:]:
        total = total + jnp.floor(v * scale + 0.5)
    q, e = encode(rotate(total * (peak / level), inner[...], rows[...]), None)
    out[:, 0:KV] = q
    out[:, KV : KV + 128] = jnp.broadcast_to(e, (16, 128)).astype(I32).astype(I16)


def finish_kernel(q, signs, out):
    e = to_float(q[:, KV : KV + 128])[:, 0:1]
    out[...] = signs[...].astype(F32) * (to_float(q[:, 0:KV]) * power(e))


def input_grad_kernel(at, c, w_own, w_oth, out, w):
    for j in range(4):
        chip = ((at[1] + 4 - j) % 4) * 256
        for z in range(NZ):
            w[pl.ds(pl.multiple_of(chip + z * 32 + at[2] * 16, 16), 16), :] = w_own[z, j, 0]
            w[pl.ds(pl.multiple_of(chip + z * 32 + 16 - at[2] * 16, 16), 16), :] = w_oth[z, j, 0]
    out[...] = lax.dot_general(c[...], w[...], (((1,), (1,)), ((), ())), preferred_element_type=F32).astype(BF16)


def tie_kernel(w, after, out):
    del w, after, out


def tie(v, after):
    return pl.pallas_call(
        tie_kernel,
        out_shape=jax.ShapeDtypeStruct(v.shape, v.dtype),
        in_specs=[pl.BlockSpec(memory_space=pl.ANY)] * 2,
        out_specs=pl.BlockSpec(memory_space=pl.ANY),
        input_output_aliases={0: 0},
        name="tie",
    )(v, after)


def params(limit=VMEM):
    return pltpu.CompilerParams(vmem_limit_bytes=limit)


def cost(flops, moved):
    return pl.CostEstimate(flops=int(flops), bytes_accessed=int(moved), transcendentals=0)


def whole(shape):
    return pl.BlockSpec(shape, lambda *_: (0,) * len(shape))


def shift(size, s):
    return [(k, (k + s) % size) for k in range(size)]


def shards(activations, cotangent, value_weights, sign_flips, level_count):
    core = lax.axis_index("core").astype(I32)
    x, y = lax.axis_index("x").astype(I32), lax.axis_index("y").astype(I32)
    sds = jax.ShapeDtypeStruct
    anywhere = pl.BlockSpec(memory_space=pl.ANY)
    in_hbm = lambda v: pltpu.with_memory_space_constraint(v, pltpu.HBM)
    in_vmem = pl.BlockSpec(memory_space=pltpu.VMEM)

    def send(v, axis, s):
        return lax.ppermute(v, "xy"[axis], shift((NX, NY)[axis], s))

    ids = []
    for axis in range(2):
        for dp in range(4):
            for dq in range(4):
                tx = (x + (dq if axis else dp)) % NX
                ty = (y + (dp if axis else dq)) % NY
                ids.append(2 * (tx * NY + ty) + axis)
    idx = jnp.stack(ids).astype(I32)

    z = lax.axis_index("z").astype(I32)

    def spread(piece, axis):
        return [lax.ppermute(piece, axis, shift(4, s)) for s in (1, 2, 3)]

    piece = lax.dynamic_slice_in_dim(value_weights, (2 * z + core) * 16, 16, 0)
    round1 = spread(piece, "x")

    def operands(where):
        tiles = [pl.BlockSpec((TOK, 128), lambda k, ids, t=t: (0, ids[where(k) + t])) for t in range(4)]
        return tiles + [whole((TOK, KV))]

    inputs = (activations,) * 4 + (cotangent,)
    message = pltpu.HBM((272, KV), I16)
    mm = 2 * 1024 * 1024 * 512

    up1x, down1x, up1y, down1y, ce = pl.pallas_call(
        far_kernel,
        out_shape=(message,) * 4 + (sds((8, KV), F32),),
        grid_spec=pltpu.PrefetchScalarGridSpec(
            num_scalar_prefetch=1,
            grid=(2,),
            in_specs=operands(lambda k: 16 * k + 8),
            out_specs=(whole((272, KV)),) * 4 + (whole((8, KV)),),
        ),
        compiler_params=params(),
        cost_estimate=cost(mm, 6 << 20),
        name="far",
    )(idx, *inputs)
    got1 = [send(up1x, 0, 1), send(down1x, 0, -1), send(up1y, 1, 1), send(down1y, 1, -1)]

    piece = jnp.concatenate([piece, tie(round1[0], up1x)] + round1[1:], 0)
    piece = jnp.concatenate([piece] + spread(piece, "y"), 0)
    w_own = lax.all_gather(piece, "z", axis=0, tiled=True)

    up2x, down2x, up2y, down2y, keep_near = pl.pallas_call(
        near_kernel,
        out_shape=(message,) * 4 + (sds((1024, KV), F32),),
        grid_spec=pltpu.PrefetchScalarGridSpec(
            num_scalar_prefetch=1,
            grid=(4,),
            in_specs=operands(lambda k: 16 * (k // 2) + 4 + 8 * (k % 2)) + [whole((8, KV))],
            out_specs=(whole((272, KV)),) * 4 + (pl.BlockSpec((256, KV), lambda k, ids: (k, 0)),),
        ),
        compiler_params=params(),
        cost_estimate=cost(2 * mm, 11 << 20),
        name="near",
    )(idx, *inputs, ce)
    got2 = [send(up2x, 0, 1), send(down2x, 0, -1), send(up2y, 1, 1), send(down2y, 1, -1)]

    keep = pl.pallas_call(
        own_kernel,
        out_shape=sds((1024, KV), F32),
        grid_spec=pltpu.PrefetchScalarGridSpec(
            num_scalar_prefetch=1,
            grid=(2,),
            in_specs=operands(lambda k: 16 * k),
            out_specs=pl.BlockSpec((512, KV), lambda k, ids: (k, 0)),
        ),
        compiler_params=params(SMALL),
        cost_estimate=cost(mm, 8 << 20),
        name="own",
    )(idx, *inputs)

    up3x, down3x, up3y, down3y = pl.pallas_call(
        relay_kernel,
        out_shape=(message,) * 4,
        grid=(4,),
        in_specs=[pl.BlockSpec((256, KV), lambda k: (k, 0)), whole((8, KV))] + [whole((272, KV))] * 4,
        out_specs=(whole((272, KV)),) * 4,
        compiler_params=params(SMALL),
        cost_estimate=cost(1 << 20, 8 << 20),
        name="relay",
    )(keep_near, ce, *got1)
    got3 = [send(up3x, 0, 1), send(down3x, 0, -1), send(up3y, 1, 1), send(down3y, 1, -1)]

    parts = pl.pallas_call(
        cross_kernel,
        out_shape=((pltpu.HBM((128, KV), F32),) + (pltpu.HBM((144, KV), I16),) * 3) * 2,
        grid=(2,),
        in_specs=[pl.BlockSpec((512, KV), lambda k: (k, 0)), whole((8, KV))] + [whole((272, KV))] * 8,
        out_specs=((whole((128, KV)),) + (whole((144, KV)),) * 3) * 2,
        compiler_params=params(SMALL),
        cost_estimate=cost(1 << 20, 12 << 20),
        name="cross",
    )(keep, ce, got2[0], got2[1], got3[0], got3[1], got2[2], got2[3], got3[2], got3[3])
    own_x, x1, x2, x3, own_y, y1, y2, y3 = parts
    last = [send(x1, 1, 1), send(x2, 1, 2), send(x3, 1, -1), send(y1, 0, 1), send(y2, 0, 2), send(y3, 0, -1)]

    inner = jnp.asarray(hadamard(128), BF16)
    quad = hadamard(4)
    spun = pl.pallas_call(
        rotate_kernel,
        out_shape=sds((256, KV + 128), I16),
        in_specs=[in_vmem] * 11,
        out_specs=in_vmem,
        compiler_params=params(SMALL),
        cost_estimate=cost(1 << 28, 4 << 20),
        name="rotate",
    )(in_hbm(own_x), in_hbm(own_y), *last, sign_flips, inner, jnp.asarray(np.kron(np.eye(32), quad), BF16))
    groups = lax.all_to_all(spun, ("z", "core"), 0, 0, tiled=True)

    w_own = tie(w_own, spun)
    w_oth = lax.ppermute(w_own, "core", shift(NC, 1))
    place = jnp.stack([x, y, core]).astype(I32)
    w_block = pl.BlockSpec((NZ, 4, 1, 16, KV), lambda k, at: (0, 0, k, 0, 0))
    input_grad = pl.pallas_call(
        input_grad_kernel,
        out_shape=pltpu.HBM((TOK, 4096), BF16),
        grid_spec=pltpu.PrefetchScalarGridSpec(
            num_scalar_prefetch=1,
            grid=(4,),
            in_specs=[whole((TOK, KV)), w_block, w_block],
            out_specs=pl.BlockSpec((TOK, 1024), lambda k, at: (0, (at[0] + 4 - k) % 4)),
            scratch_shapes=[pltpu.VMEM((1024, KV), BF16)],
        ),
        compiler_params=params(SMALL),
        cost_estimate=cost(4 * mm, 13 << 20),
        name="input_grad",
    )(place, cotangent, w_own.reshape(NZ, 4, 4, 16, KV), w_oth.reshape(NZ, 4, 4, 16, KV))

    back = pl.pallas_call(
        levels_kernel,
        out_shape=sds((16, KV + 128), I16),
        in_specs=[pl.BlockSpec(memory_space=pltpu.SMEM)] + [in_vmem] * 3 + [anywhere],
        out_specs=in_vmem,
        compiler_params=params(SMALL),
        cost_estimate=cost(1 << 26, 1 << 20),
        name="levels",
    )(level_count.reshape(1), groups, inner, jnp.asarray(np.kron(np.eye(4), quad), BF16), in_hbm(input_grad))
    gathered = lax.all_gather(back, ("z", "core"), axis=0, tiled=True)
    weight_grad = pl.pallas_call(
        finish_kernel,
        out_shape=sds((256, KV), F32),
        in_specs=[in_vmem] * 2,
        out_specs=in_vmem,
        compiler_params=params(SMALL),
        cost_estimate=cost(1 << 20, 3 << 20),
        name="finish",
    )(gathered, sign_flips)
    return (input_grad, weight_grad)


def solution(mesh):
    torus = Mesh(mesh.devices.reshape(NZ, NC, NX, NY), AXES)
    rows = P(AXES, None)
    part = P(("x", "y"), None)
    return jax.shard_map(
        shards,
        mesh=torus,
        in_specs=(rows, rows, part, part, P()),
        out_specs=(rows, part),
        check_vma=False,
    )
```

```python
import jax
import jax.numpy as jnp
import numpy as np
from jax import lax
from jax.experimental import pallas as pl
from jax.experimental.pallas import tpu as pltpu
from jax.sharding import Mesh, PartitionSpec as P

NZ, NC, NX, NY = 8, 2, 4, 4
AXES = ("z", "core", "x", "y")
KV = 1024
TOK = 512
F32, BF16, I16, I32 = jnp.float32, jnp.bfloat16, jnp.int16, jnp.int32
VMEM = 56 * 1024 * 1024
SMALL = 24 * 1024 * 1024


def hadamard(size):
    positions = np.arange(size)
    common = positions[:, None] & positions[None, :]
    parity = np.zeros((size, size), np.int64)
    for bit in range(16):
        parity += (common >> bit) & 1
    return (1 - 2 * (parity & 1)).astype(np.float32)


def power(e):
    return jnp.exp2(e * 0.125)


def step_of(top, low):
    return jnp.ceil(jnp.log2(jnp.maximum(top, low)) * 8.0)


def encode(v, ce):
    u = v if ce is None else v * power(-ce)
    e = step_of(jnp.max(jnp.abs(u), axis=1, keepdims=True), 1e-30) - 119.0
    q = jnp.floor(u * power(-e) + 0.5)
    return q.astype(I32).astype(I16), e


def to_float(q):
    return q.astype(I32).astype(F32)


def eye():
    return lax.broadcasted_iota(I32, (128, 128), 0) == lax.broadcasted_iota(I32, (128, 128), 1)


def to_lanes(col):
    return jnp.sum(jnp.where(eye(), col, 0.0), axis=0, keepdims=True)


def to_rows(row):
    return jnp.sum(jnp.where(eye(), row, 0.0), axis=1, keepdims=True)


def write(msg, v, ce):
    count = v.shape[0]
    q, e = encode(v, ce)
    msg[0:count, :] = q
    parts = [to_lanes(e[k : k + 128]) for k in range(0, count, 128)]
    line = jnp.concatenate(parts + [jnp.zeros((1, KV - count), F32)], 1)
    row = lax.broadcasted_iota(I32, (16, KV), 0)
    extra = jnp.where(row == 0, line, jnp.where(row == 1, ce, 0.0))
    msg[count : count + 16, :] = extra.astype(I32).astype(I16)


def steps_in(msg):
    count = msg.shape[0] - 16
    return to_float(msg[count : count + 16, :])


def read(msg):
    count = msg.shape[0] - 16
    extra = steps_in(msg)
    e = jnp.concatenate([to_rows(extra[0:1, k : k + 128]) for k in range(0, count, 128)], 0)
    return to_float(msg[0:count, :]) * power(e) * power(extra[1:2, :])


def product(tiles, c):
    a = jnp.concatenate([t[...] for t in tiles], 1)
    return lax.dot_general(a, c[...], (((0,), (0,)), ((), ())), preferred_element_type=F32)


def column_steps(c):
    top = jnp.max(jnp.abs(c.astype(F32)), axis=0, keepdims=True)
    return jnp.clip(step_of(top, 1e-30), -800.0, 800.0)


def half(v, number):
    return jnp.concatenate([v[k + 64 * number : k + 64 * number + 64] for k in range(0, v.shape[0], 128)], 0)


def far_kernel(idx, t0, t1, t2, t3, c, *refs):
    up, down, ce = refs[-3:]
    ce[...] = jnp.broadcast_to(column_steps(c[...]), (8, KV))
    p = product((t0, t1, t2, t3), c)
    write(up, half(p, 0), ce[0:1, :])
    write(down, half(p, 1), ce[0:1, :])


def near_kernel(idx, t0, t1, t2, t3, c, ce, up_x, down_x, up_y, down_y, keep):
    p = product((t0, t1, t2, t3), c)
    for step, msg in enumerate((up_x, down_x, up_y, down_y)):

        @pl.when(pl.program_id(0) == step)
        def _(step=step, msg=msg):
            kept = step % 2
            keep[...] = half(p, kept)
            write(msg, half(p, 1 - kept), ce[0:1, :])


def own_kernel(idx, t0, t1, t2, t3, c, keep):
    keep[...] = product((t0, t1, t2, t3), c)


def relay_kernel(keep, ce, *refs):
    for step in range(4):

        @pl.when(pl.program_id(0) == step)
        def _(got=refs[step], msg=refs[4 + step]):
            write(msg, keep[...] + read(got), jnp.maximum(ce[0:1, :], steps_in(got)[1:2, :]))


def cross_kernel(keep, ce, *refs):
    for axis in range(2):

        @pl.when(pl.program_id(0) == axis)
        def _(got=refs[4 * axis : 4 * axis + 4], out=refs[8 + 4 * axis : 12 + 4 * axis]):
            up2, down2, up3, down3 = got
            ce_all = ce[0:1, :]
            for msg in got:
                ce_all = jnp.maximum(ce_all, steps_in(msg)[1:2, :])
            first, last = read(up3) + read(down2), read(up2) + read(down3)
            for t in range(4):
                rows = slice(t * 64, t * 64 + 64)
                total = keep[t * 128 : t * 128 + 128, :] + jnp.concatenate([first[rows], last[rows]], 0)
                if t == 0:
                    out[0][...] = total
                else:
                    write(out[t], total, ce_all)


def split_dot(x, m):
    hi = x.astype(BF16)
    rest = x - hi.astype(F32)
    mid = rest.astype(BF16)
    lo = (rest - mid.astype(F32)).astype(BF16)
    dot = lambda a: jnp.dot(a, m, preferred_element_type=F32)
    return dot(hi) + (dot(mid) + dot(lo))


def split_dot_left(m, x):
    hi = x.astype(BF16)
    rest = x - hi.astype(F32)
    mid = rest.astype(BF16)
    lo = (rest - mid.astype(F32)).astype(BF16)
    dot = lambda a: jnp.dot(m, a, preferred_element_type=F32)
    return dot(hi) + (dot(mid) + dot(lo))


def rotate(v, inner, rows):
    tiles = [v[:, k * 128 : (k + 1) * 128] for k in range(8)]
    for bit in (1, 2, 4):
        tiles = [tiles[k ^ bit] - tiles[k] if k & bit else tiles[k] + tiles[k ^ bit] for k in range(8)]
    mixed = jnp.concatenate([split_dot(t, inner) for t in tiles], 1)
    return split_dot_left(rows, mixed) * (1.0 / 64.0)


def rotate_kernel(own_x, own_y, x1, x2, x3, y1, y2, y3, signs, inner, rows, out):
    for k, (own, msgs) in enumerate(((own_x, (x1, x2, x3)), (own_y, (y1, y2, y3)))):
        here = slice(k * 128, k * 128 + 128)
        total = own[...]
        for msg in msgs:
            total = total + read(msg)
        q, e = encode(rotate(total * signs[here, :].astype(F32), inner[...], rows[...]), None)
        out[here, 0:KV] = q
        out[here, KV : KV + 128] = jnp.broadcast_to(e, (128, 128)).astype(I32).astype(I16)


def levels_kernel(count, x, inner, rows, after, out):
    level = count[0].astype(F32)

    def group(g):
        q = x[g * 16 : g * 16 + 16, :]
        e = to_float(q[:, KV : KV + 128])[:, 0:1]
        return to_float(q[:, 0:KV]) * power(e)

    groups = [group(g) for g in range(NZ * NC)]
    top = jnp.abs(groups[0])
    for v in groups[1:]:
        top = jnp.maximum(top, jnp.abs(v))
    top = jnp.max(top, axis=1, keepdims=True)
    block = lax.shift_right_logical(lax.broadcasted_iota(I32, (16, 1), 0), 2)
    peak = jnp.zeros((16, 1), F32)
    for b in range(4):
        peak = jnp.where(block == b, jnp.max(jnp.where(block == b, top, 0.0), axis=0, keepdims=True), peak)
    peak = peak + 1e-06
    scale = level / peak
    total = jnp.floor(groups[0] * scale + 0.5)
    for v in groups[1:]:
        total = total + jnp.floor(v * scale + 0.5)
    q, e = encode(rotate(total * (peak / level), inner[...], rows[...]), None)
    out[:, 0:KV] = q
    out[:, KV : KV + 128] = jnp.broadcast_to(e, (16, 128)).astype(I32).astype(I16)


def finish_kernel(q, signs, out):
    e = to_float(q[:, KV : KV + 128])[:, 0:1]
    out[...] = signs[...].astype(F32) * (to_float(q[:, 0:KV]) * power(e))


def input_grad_kernel(at, c, w_own, w_oth, out, w):
    for j in range(4):
        chip = ((at[1] + 4 - j) % 4) * 256
        for z in range(NZ):
            w[pl.ds(pl.multiple_of(chip + z * 32 + at[2] * 16, 16), 16), :] = w_own[z, j, 0]
            w[pl.ds(pl.multiple_of(chip + z * 32 + 16 - at[2] * 16, 16), 16), :] = w_oth[z, j, 0]
    out[...] = lax.dot_general(c[...], w[...], (((1,), (1,)), ((), ())), preferred_element_type=F32).astype(BF16)


def tie_kernel(w, after, out):
    del w, after, out


def tie(v, after):
    return pl.pallas_call(
        tie_kernel,
        out_shape=jax.ShapeDtypeStruct(v.shape, v.dtype),
        in_specs=[pl.BlockSpec(memory_space=pl.ANY)] * 2,
        out_specs=pl.BlockSpec(memory_space=pl.ANY),
        input_output_aliases={0: 0},
        name="tie",
    )(v, after)


def params(limit=VMEM):
    return pltpu.CompilerParams(vmem_limit_bytes=limit)


def cost(flops, moved):
    return pl.CostEstimate(flops=int(flops), bytes_accessed=int(moved), transcendentals=0)


def whole(shape):
    return pl.BlockSpec(shape, lambda *_: (0,) * len(shape))


def shift(size, s):
    return [(k, (k + s) % size) for k in range(size)]


def shards(activations, cotangent, value_weights, sign_flips, level_count):
    core = lax.axis_index("core").astype(I32)
    x, y = lax.axis_index("x").astype(I32), lax.axis_index("y").astype(I32)
    sds = jax.ShapeDtypeStruct
    anywhere = pl.BlockSpec(memory_space=pl.ANY)
    in_hbm = lambda v: pltpu.with_memory_space_constraint(v, pltpu.HBM)
    in_vmem = pl.BlockSpec(memory_space=pltpu.VMEM)

    def send(v, axis, s):
        return lax.ppermute(v, "xy"[axis], shift((NX, NY)[axis], s))

    ids = []
    for axis in range(2):
        for dp in range(4):
            for dq in range(4):
                tx = (x + (dq if axis else dp)) % NX
                ty = (y + (dp if axis else dq)) % NY
                ids.append(2 * (tx * NY + ty) + axis)
    idx = jnp.stack(ids).astype(I32)

    z = lax.axis_index("z").astype(I32)

    def spread(piece, axis):
        return [lax.ppermute(piece, axis, shift(4, s)) for s in (1, 2, 3)]

    piece = lax.dynamic_slice_in_dim(value_weights, (2 * z + core) * 16, 16, 0)
    round1 = spread(piece, "x")

    def operands(where):
        tiles = [pl.BlockSpec((TOK, 128), lambda k, ids, t=t: (0, ids[where(k) + t])) for t in range(4)]
        return tiles + [whole((TOK, KV))]

    inputs = (in_hbm(activations),) * 4 + (in_hbm(cotangent),)
    message = pltpu.HBM((272, KV), I16)
    mm = 2 * 1024 * 1024 * 512

    def far(axis, *after):
        return pl.pallas_call(
            far_kernel,
            out_shape=(message, message, sds((8, KV), F32)),
            grid_spec=pltpu.PrefetchScalarGridSpec(
                num_scalar_prefetch=1,
                grid=(1,),
                in_specs=operands(lambda k: 16 * axis + 8) + [anywhere] * len(after),
                out_specs=(whole((272, KV)), whole((272, KV)), whole((8, KV))),
            ),
            compiler_params=params(SMALL),
            cost_estimate=cost(mm // 2, 3 << 20),
            name="far",
        )(idx, *inputs, *after)

    up1x, down1x, ce = far(0)
    piece = jnp.concatenate([piece, tie(round1[0], up1x)] + round1[1:], 0)
    round2 = spread(piece, "y")
    up1y, down1y, _ = far(1, piece)
    piece = jnp.concatenate([piece, tie(round2[0], up1y)] + round2[1:], 0)
    w_own = lax.all_gather(piece, "z", axis=0, tiled=True)
    got1 = [send(up1x, 0, 1), send(down1x, 0, -1), send(up1y, 1, 1), send(down1y, 1, -1)]

    up2x, down2x, up2y, down2y, keep_near = pl.pallas_call(
        near_kernel,
        out_shape=(message,) * 4 + (sds((1024, KV), F32),),
        grid_spec=pltpu.PrefetchScalarGridSpec(
            num_scalar_prefetch=1,
            grid=(4,),
            in_specs=operands(lambda k: 16 * (k // 2) + 4 + 8 * (k % 2)) + [whole((8, KV))],
            out_specs=(whole((272, KV)),) * 4 + (pl.BlockSpec((256, KV), lambda k, ids: (k, 0)),),
        ),
        compiler_params=params(SMALL),
        cost_estimate=cost(2 * mm, 11 << 20),
        name="near",
    )(idx, *inputs, ce)
    got2 = [send(up2x, 0, 1), send(down2x, 0, -1), send(up2y, 1, 1), send(down2y, 1, -1)]

    keep = pl.pallas_call(
        own_kernel,
        out_shape=sds((1024, KV), F32),
        grid_spec=pltpu.PrefetchScalarGridSpec(
            num_scalar_prefetch=1,
            grid=(2,),
            in_specs=operands(lambda k: 16 * k),
            out_specs=pl.BlockSpec((512, KV), lambda k, ids: (k, 0)),
        ),
        compiler_params=params(SMALL),
        cost_estimate=cost(mm, 8 << 20),
        name="own",
    )(idx, *inputs)

    up3x, down3x, up3y, down3y = pl.pallas_call(
        relay_kernel,
        out_shape=(message,) * 4,
        grid=(4,),
        in_specs=[pl.BlockSpec((256, KV), lambda k: (k, 0)), whole((8, KV))] + [whole((272, KV))] * 4,
        out_specs=(whole((272, KV)),) * 4,
        compiler_params=params(SMALL),
        cost_estimate=cost(1 << 20, 8 << 20),
        name="relay",
    )(keep_near, ce, *got1)
    got3 = [send(up3x, 0, 1), send(down3x, 0, -1), send(up3y, 1, 1), send(down3y, 1, -1)]

    parts = pl.pallas_call(
        cross_kernel,
        out_shape=((pltpu.HBM((128, KV), F32),) + (pltpu.HBM((144, KV), I16),) * 3) * 2,
        grid=(2,),
        in_specs=[pl.BlockSpec((512, KV), lambda k: (k, 0)), whole((8, KV))] + [whole((272, KV))] * 8,
        out_specs=((whole((128, KV)),) + (whole((144, KV)),) * 3) * 2,
        compiler_params=params(SMALL),
        cost_estimate=cost(1 << 20, 12 << 20),
        name="cross",
    )(keep, ce, got2[0], got2[1], got3[0], got3[1], got2[2], got2[3], got3[2], got3[3])
    own_x, x1, x2, x3, own_y, y1, y2, y3 = parts
    last = [send(x1, 1, 1), send(x2, 1, 2), send(x3, 1, -1), send(y1, 0, 1), send(y2, 0, 2), send(y3, 0, -1)]

    inner = jnp.asarray(hadamard(128), BF16)
    quad = hadamard(4)
    spun = pl.pallas_call(
        rotate_kernel,
        out_shape=sds((256, KV + 128), I16),
        in_specs=[in_vmem] * 11,
        out_specs=in_vmem,
        compiler_params=params(SMALL),
        cost_estimate=cost(1 << 28, 4 << 20),
        name="rotate",
    )(in_hbm(own_x), in_hbm(own_y), *last, sign_flips, inner, jnp.asarray(np.kron(np.eye(32), quad), BF16))
    groups = lax.all_to_all(spun, ("z", "core"), 0, 0, tiled=True)

    w_own = tie(w_own, spun)
    w_oth = lax.ppermute(w_own, "core", shift(NC, 1))
    place = jnp.stack([x, y, core]).astype(I32)
    w_block = pl.BlockSpec((NZ, 4, 1, 16, KV), lambda k, at: (0, 0, k, 0, 0))
    input_grad = pl.pallas_call(
        input_grad_kernel,
        out_shape=pltpu.HBM((TOK, 4096), BF16),
        grid_spec=pltpu.PrefetchScalarGridSpec(
            num_scalar_prefetch=1,
            grid=(4,),
            in_specs=[whole((TOK, KV)), w_block, w_block],
            out_specs=pl.BlockSpec((TOK, 1024), lambda k, at: (0, (at[0] + 4 - k) % 4)),
            scratch_shapes=[pltpu.VMEM((1024, KV), BF16)],
        ),
        compiler_params=params(SMALL),
        cost_estimate=cost(4 * mm, 13 << 20),
        name="input_grad",
    )(place, cotangent, w_own.reshape(NZ, 4, 4, 16, KV), w_oth.reshape(NZ, 4, 4, 16, KV))

    back = pl.pallas_call(
        levels_kernel,
        out_shape=sds((16, KV + 128), I16),
        in_specs=[pl.BlockSpec(memory_space=pltpu.SMEM)] + [in_vmem] * 3 + [anywhere],
        out_specs=in_vmem,
        compiler_params=params(SMALL),
        cost_estimate=cost(1 << 26, 1 << 20),
        name="levels",
    )(level_count.reshape(1), groups, inner, jnp.asarray(np.kron(np.eye(4), quad), BF16), in_hbm(input_grad))
    gathered = lax.all_gather(back, ("z", "core"), axis=0, tiled=True)
    weight_grad = pl.pallas_call(
        finish_kernel,
        out_shape=sds((256, KV), F32),
        in_specs=[in_vmem] * 2,
        out_specs=in_vmem,
        compiler_params=params(SMALL),
        cost_estimate=cost(1 << 20, 3 << 20),
        name="finish",
    )(gathered, sign_flips)
    return (input_grad, weight_grad)


def solution(mesh):
    torus = Mesh(mesh.devices.reshape(NZ, NC, NX, NY), AXES)
    rows = P(AXES, None)
    part = P(("x", "y"), None)
    return jax.shard_map(
        shards,
        mesh=torus,
        in_specs=(rows, rows, part, part, P()),
        out_specs=(rows, part),
        check_vma=False,
    )
```

```python
import jax
import jax.numpy as jnp
import numpy as np
from jax import lax
from jax.experimental import pallas as pl
from jax.experimental.pallas import tpu as pltpu
from jax.sharding import Mesh, PartitionSpec as P

NZ, NC, NX, NY = 8, 2, 4, 4
AXES = ("z", "core", "x", "y")
KV = 1024
TOK = 512
F32, BF16, I16, I32 = jnp.float32, jnp.bfloat16, jnp.int16, jnp.int32
VMEM = 56 * 1024 * 1024
SMALL = 24 * 1024 * 1024


def hadamard(size):
    positions = np.arange(size)
    common = positions[:, None] & positions[None, :]
    parity = np.zeros((size, size), np.int64)
    for bit in range(16):
        parity += (common >> bit) & 1
    return (1 - 2 * (parity & 1)).astype(np.float32)


def power(e):
    return jnp.exp2(e * 0.125)


def step_of(top, low):
    return jnp.ceil(jnp.log2(jnp.maximum(top, low)) * 8.0)


def encode(v, ce):
    u = v if ce is None else v * power(-ce)
    e = step_of(jnp.max(jnp.abs(u), axis=1, keepdims=True), 1e-30) - 119.0
    q = jnp.floor(u * power(-e) + 0.5)
    return q.astype(I32).astype(I16), e


def to_float(q):
    return q.astype(I32).astype(F32)


def eye():
    return lax.broadcasted_iota(I32, (128, 128), 0) == lax.broadcasted_iota(I32, (128, 128), 1)


def to_lanes(col):
    return jnp.sum(jnp.where(eye(), col, 0.0), axis=0, keepdims=True)


def to_rows(row):
    return jnp.sum(jnp.where(eye(), row, 0.0), axis=1, keepdims=True)


def write(msg, v, ce):
    count = v.shape[0]
    q, e = encode(v, ce)
    msg[0:count, :] = q
    parts = [to_lanes(e[k : k + 128]) for k in range(0, count, 128)]
    line = jnp.concatenate(parts + [jnp.zeros((1, KV - count), F32)], 1)
    row = lax.broadcasted_iota(I32, (16, KV), 0)
    extra = jnp.where(row == 0, line, jnp.where(row == 1, ce, 0.0))
    msg[count : count + 16, :] = extra.astype(I32).astype(I16)


def steps_in(msg):
    count = msg.shape[0] - 16
    return to_float(msg[count : count + 16, :])


def read(msg):
    count = msg.shape[0] - 16
    extra = steps_in(msg)
    e = jnp.concatenate([to_rows(extra[0:1, k : k + 128]) for k in range(0, count, 128)], 0)
    return to_float(msg[0:count, :]) * power(e) * power(extra[1:2, :])


def product(tiles, c):
    a = jnp.concatenate([t[...] for t in tiles], 1)
    return lax.dot_general(a, c[...], (((0,), (0,)), ((), ())), preferred_element_type=F32)


def column_steps(c):
    top = jnp.max(jnp.abs(c.astype(F32)), axis=0, keepdims=True)
    return jnp.clip(step_of(top, 1e-30), -800.0, 800.0)


def half(v, number):
    return jnp.concatenate([v[k + 64 * number : k + 64 * number + 64] for k in range(0, v.shape[0], 128)], 0)


def far_kernel(idx, t0, t1, t2, t3, c, *refs):
    up, down, ce = refs[-3:]
    ce[...] = jnp.broadcast_to(column_steps(c[...]), (8, KV))
    p = product((t0, t1, t2, t3), c)
    write(up, half(p, 0), ce[0:1, :])
    write(down, half(p, 1), ce[0:1, :])


def near_kernel(idx, t0, t1, t2, t3, c, ce, up_x, down_x, up_y, down_y, keep):
    p = product((t0, t1, t2, t3), c)
    for step, msg in enumerate((up_x, down_x, up_y, down_y)):

        @pl.when(pl.program_id(0) == step)
        def _(step=step, msg=msg):
            kept = step % 2
            keep[...] = half(p, kept)
            write(msg, half(p, 1 - kept), ce[0:1, :])


def own_kernel(idx, t0, t1, t2, t3, c, keep):
    keep[...] = product((t0, t1, t2, t3), c)


def relay_kernel(keep, ce, *refs):
    for step in range(4):

        @pl.when(pl.program_id(0) == step)
        def _(got=refs[step], msg=refs[4 + step]):
            write(msg, keep[...] + read(got), jnp.maximum(ce[0:1, :], steps_in(got)[1:2, :]))


def cross_kernel(keep, ce, *refs):
    for axis in range(2):

        @pl.when(pl.program_id(0) == axis)
        def _(got=refs[4 * axis : 4 * axis + 4], out=refs[8 + 4 * axis : 12 + 4 * axis]):
            up2, down2, up3, down3 = got
            ce_all = ce[0:1, :]
            for msg in got:
                ce_all = jnp.maximum(ce_all, steps_in(msg)[1:2, :])
            first, last = read(up3) + read(down2), read(up2) + read(down3)
            for t in range(4):
                rows = slice(t * 64, t * 64 + 64)
                total = keep[t * 128 : t * 128 + 128, :] + jnp.concatenate([first[rows], last[rows]], 0)
                if t == 0:
                    out[0][...] = total
                else:
                    write(out[t], total, ce_all)


def split_dot(x, m):
    hi = x.astype(BF16)
    rest = x - hi.astype(F32)
    mid = rest.astype(BF16)
    lo = (rest - mid.astype(F32)).astype(BF16)
    dot = lambda a: jnp.dot(a, m, preferred_element_type=F32)
    return dot(hi) + (dot(mid) + dot(lo))


def split_dot_left(m, x):
    hi = x.astype(BF16)
    rest = x - hi.astype(F32)
    mid = rest.astype(BF16)
    lo = (rest - mid.astype(F32)).astype(BF16)
    dot = lambda a: jnp.dot(m, a, preferred_element_type=F32)
    return dot(hi) + (dot(mid) + dot(lo))


def rotate(v, inner, rows):
    tiles = [v[:, k * 128 : (k + 1) * 128] for k in range(8)]
    for bit in (1, 2, 4):
        tiles = [tiles[k ^ bit] - tiles[k] if k & bit else tiles[k] + tiles[k ^ bit] for k in range(8)]
    mixed = jnp.concatenate([split_dot(t, inner) for t in tiles], 1)
    return split_dot_left(rows, mixed) * (1.0 / 64.0)


def rotate_kernel(own, n1, n2, n3, signs, inner, rows, *refs):
    out = refs[-1]
    total = own[...]
    for msg in (n1, n2, n3):
        total = total + read(msg)
    q, e = encode(rotate(total * signs[...].astype(F32), inner[...], rows[...]), None)
    out[:, 0:KV] = q
    out[:, KV : KV + 128] = jnp.broadcast_to(e, (128, 128)).astype(I32).astype(I16)


def levels_kernel(count, x, inner, rows, after, out):
    level = count[0].astype(F32)

    def group(g):
        q = x[g * 16 : g * 16 + 16, :]
        e = to_float(q[:, KV : KV + 128])[:, 0:1]
        return to_float(q[:, 0:KV]) * power(e)

    groups = [group(g) for g in range(NZ * NC)]
    top = jnp.abs(groups[0])
    for v in groups[1:]:
        top = jnp.maximum(top, jnp.abs(v))
    top = jnp.max(top, axis=1, keepdims=True)
    block = lax.shift_right_logical(lax.broadcasted_iota(I32, (16, 1), 0), 2)
    peak = jnp.zeros((16, 1), F32)
    for b in range(4):
        peak = jnp.where(block == b, jnp.max(jnp.where(block == b, top, 0.0), axis=0, keepdims=True), peak)
    peak = peak + 1e-06
    scale = level / peak
    total = jnp.floor(groups[0] * scale + 0.5)
    for v in groups[1:]:
        total = total + jnp.floor(v * scale + 0.5)
    q, e = encode(rotate(total * (peak / level), inner[...], rows[...]), None)
    out[:, 0:KV] = q
    out[:, KV : KV + 128] = jnp.broadcast_to(e, (16, 128)).astype(I32).astype(I16)


def finish_kernel(q, signs, out):
    e = to_float(q[:, KV : KV + 128])[:, 0:1]
    out[...] = signs[...].astype(F32) * (to_float(q[:, 0:KV]) * power(e))


def input_grad_kernel(at, c, w_own, w_oth, out, w):
    for j in range(4):
        chip = ((at[1] + 4 - j) % 4) * 256
        for z in range(NZ):
            w[pl.ds(pl.multiple_of(chip + z * 32 + at[2] * 16, 16), 16), :] = w_own[z, j, 0]
            w[pl.ds(pl.multiple_of(chip + z * 32 + 16 - at[2] * 16, 16), 16), :] = w_oth[z, j, 0]
    out[...] = lax.dot_general(c[...], w[...], (((1,), (1,)), ((), ())), preferred_element_type=F32).astype(BF16)


def tie_kernel(w, after, out):
    del w, after, out


def tie(v, after):
    return pl.pallas_call(
        tie_kernel,
        out_shape=jax.ShapeDtypeStruct(v.shape, v.dtype),
        in_specs=[pl.BlockSpec(memory_space=pl.ANY)] * 2,
        out_specs=pl.BlockSpec(memory_space=pl.ANY),
        input_output_aliases={0: 0},
        name="tie",
    )(v, after)


def params(limit=VMEM):
    return pltpu.CompilerParams(vmem_limit_bytes=limit)


def cost(flops, moved):
    return pl.CostEstimate(flops=int(flops), bytes_accessed=int(moved), transcendentals=0)


def whole(shape):
    return pl.BlockSpec(shape, lambda *_: (0,) * len(shape))


def shift(size, s):
    return [(k, (k + s) % size) for k in range(size)]


def shards(activations, cotangent, value_weights, sign_flips, level_count):
    core = lax.axis_index("core").astype(I32)
    x, y = lax.axis_index("x").astype(I32), lax.axis_index("y").astype(I32)
    sds = jax.ShapeDtypeStruct
    anywhere = pl.BlockSpec(memory_space=pl.ANY)
    in_hbm = lambda v: pltpu.with_memory_space_constraint(v, pltpu.HBM)
    in_vmem = pl.BlockSpec(memory_space=pltpu.VMEM)

    def send(v, axis, s):
        return lax.ppermute(v, "xy"[axis], shift((NX, NY)[axis], s))

    ids = []
    for axis in range(2):
        for dp in range(4):
            for dq in range(4):
                tx = (x + (dq if axis else dp)) % NX
                ty = (y + (dp if axis else dq)) % NY
                ids.append(2 * (tx * NY + ty) + axis)
    idx = jnp.stack(ids).astype(I32)

    z = lax.axis_index("z").astype(I32)

    def spread(piece, axis):
        return [lax.ppermute(piece, axis, shift(4, s)) for s in (1, 2, 3)]

    piece = lax.dynamic_slice_in_dim(value_weights, (2 * z + core) * 16, 16, 0)
    round1 = spread(piece, "x")

    def operands(where):
        tiles = [pl.BlockSpec((TOK, 128), lambda k, ids, t=t: (0, ids[where(k) + t])) for t in range(4)]
        return tiles + [whole((TOK, KV))]

    inputs = (in_hbm(activations),) * 4 + (in_hbm(cotangent),)
    message = pltpu.HBM((272, KV), I16)
    mm = 2 * 1024 * 1024 * 512

    def far(axis, *after):
        return pl.pallas_call(
            far_kernel,
            out_shape=(message, message, sds((8, KV), F32)),
            grid_spec=pltpu.PrefetchScalarGridSpec(
                num_scalar_prefetch=1,
                grid=(1,),
                in_specs=operands(lambda k: 16 * axis + 8) + [anywhere] * len(after),
                out_specs=(whole((272, KV)), whole((272, KV)), whole((8, KV))),
            ),
            compiler_params=params(SMALL),
            cost_estimate=cost(mm // 2, 3 << 20),
            name="far",
        )(idx, *inputs, *after)

    up1x, down1x, ce = far(0)
    piece = jnp.concatenate([piece, tie(round1[0], up1x)] + round1[1:], 0)
    round2 = spread(piece, "y")
    up1y, down1y, _ = far(1, piece)
    piece = jnp.concatenate([piece, tie(round2[0], up1y)] + round2[1:], 0)
    w_own = lax.all_gather(piece, "z", axis=0, tiled=True)
    got1 = [send(up1x, 0, 1), send(down1x, 0, -1), send(up1y, 1, 1), send(down1y, 1, -1)]

    up2x, down2x, up2y, down2y, keep_near = pl.pallas_call(
        near_kernel,
        out_shape=(message,) * 4 + (sds((1024, KV), F32),),
        grid_spec=pltpu.PrefetchScalarGridSpec(
            num_scalar_prefetch=1,
            grid=(4,),
            in_specs=operands(lambda k: 16 * (k // 2) + 4 + 8 * (k % 2)) + [whole((8, KV))],
            out_specs=(whole((272, KV)),) * 4 + (pl.BlockSpec((256, KV), lambda k, ids: (k, 0)),),
        ),
        compiler_params=params(SMALL),
        cost_estimate=cost(2 * mm, 11 << 20),
        name="near",
    )(idx, *inputs, ce)
    got2 = [send(up2x, 0, 1), send(down2x, 0, -1), send(up2y, 1, 1), send(down2y, 1, -1)]

    keep = pl.pallas_call(
        own_kernel,
        out_shape=sds((1024, KV), F32),
        grid_spec=pltpu.PrefetchScalarGridSpec(
            num_scalar_prefetch=1,
            grid=(2,),
            in_specs=operands(lambda k: 16 * k),
            out_specs=pl.BlockSpec((512, KV), lambda k, ids: (k, 0)),
        ),
        compiler_params=params(SMALL),
        cost_estimate=cost(mm, 8 << 20),
        name="own",
    )(idx, *inputs)

    up3x, down3x, up3y, down3y = pl.pallas_call(
        relay_kernel,
        out_shape=(message,) * 4,
        grid=(4,),
        in_specs=[pl.BlockSpec((256, KV), lambda k: (k, 0)), whole((8, KV))] + [whole((272, KV))] * 4,
        out_specs=(whole((272, KV)),) * 4,
        compiler_params=params(SMALL),
        cost_estimate=cost(1 << 20, 8 << 20),
        name="relay",
    )(keep_near, ce, *got1)
    got3 = [send(up3x, 0, 1), send(down3x, 0, -1), send(up3y, 1, 1), send(down3y, 1, -1)]

    parts = pl.pallas_call(
        cross_kernel,
        out_shape=((pltpu.HBM((128, KV), F32),) + (pltpu.HBM((144, KV), I16),) * 3) * 2,
        grid=(2,),
        in_specs=[pl.BlockSpec((512, KV), lambda k: (k, 0)), whole((8, KV))] + [whole((272, KV))] * 8,
        out_specs=((whole((128, KV)),) + (whole((144, KV)),) * 3) * 2,
        compiler_params=params(SMALL),
        cost_estimate=cost(1 << 20, 12 << 20),
        name="cross",
    )(keep, ce, got2[0], got2[1], got3[0], got3[1], got2[2], got2[3], got3[2], got3[3])
    own_x, x1, x2, x3, own_y, y1, y2, y3 = parts
    last = [send(x1, 1, 1), send(x2, 1, 2), send(x3, 1, -1), send(y1, 0, 1), send(y2, 0, 2), send(y3, 0, -1)]

    inner = jnp.asarray(hadamard(128), BF16)
    quad = hadamard(4)
    eights = jnp.asarray(np.kron(np.eye(32), quad), BF16)

    def rotated(axis, own, msgs, *before):
        return pl.pallas_call(
            rotate_kernel,
            out_shape=pltpu.HBM((256, KV + 128), I16),
            grid=(1,),
            in_specs=[whole((128, KV))]
            + [whole((144, KV))] * 3
            + [pl.BlockSpec((128, KV), lambda k: (axis, 0)), whole((128, 128)), whole((128, 128))]
            + [anywhere] * len(before),
            out_specs=pl.BlockSpec((128, KV + 128), lambda k: (axis, 0)),
            input_output_aliases={7: 0} if before else {},
            compiler_params=params(SMALL),
            cost_estimate=cost(1 << 27, 2 << 20),
            name="rotate",
        )(in_hbm(own), *msgs, sign_flips, inner, eights, *before)

    spun = rotated(1, own_y, last[3:], rotated(0, own_x, last[:3]))
    groups = lax.all_to_all(spun, ("z", "core"), 0, 0, tiled=True)

    w_own = tie(w_own, spun)
    w_oth = lax.ppermute(w_own, "core", shift(NC, 1))
    place = jnp.stack([x, y, core]).astype(I32)
    w_block = pl.BlockSpec((NZ, 4, 1, 16, KV), lambda k, at: (0, 0, k, 0, 0))
    input_grad = pl.pallas_call(
        input_grad_kernel,
        out_shape=pltpu.HBM((TOK, 4096), BF16),
        grid_spec=pltpu.PrefetchScalarGridSpec(
            num_scalar_prefetch=1,
            grid=(4,),
            in_specs=[whole((TOK, KV)), w_block, w_block],
            out_specs=pl.BlockSpec((TOK, 1024), lambda k, at: (0, (at[0] + 4 - k) % 4)),
            scratch_shapes=[pltpu.VMEM((1024, KV), BF16)],
        ),
        compiler_params=params(SMALL),
        cost_estimate=cost(4 * mm, 13 << 20),
        name="input_grad",
    )(place, cotangent, w_own.reshape(NZ, 4, 4, 16, KV), w_oth.reshape(NZ, 4, 4, 16, KV))

    back = pl.pallas_call(
        levels_kernel,
        out_shape=sds((16, KV + 128), I16),
        in_specs=[pl.BlockSpec(memory_space=pltpu.SMEM)] + [in_vmem] * 3 + [anywhere],
        out_specs=in_vmem,
        compiler_params=params(SMALL),
        cost_estimate=cost(1 << 26, 1 << 20),
        name="levels",
    )(level_count.reshape(1), groups, inner, jnp.asarray(np.kron(np.eye(4), quad), BF16), in_hbm(input_grad))
    gathered = lax.all_gather(back, ("z", "core"), axis=0, tiled=True)
    weight_grad = pl.pallas_call(
        finish_kernel,
        out_shape=sds((256, KV), F32),
        in_specs=[in_vmem] * 2,
        out_specs=in_vmem,
        compiler_params=params(SMALL),
        cost_estimate=cost(1 << 20, 3 << 20),
        name="finish",
    )(gathered, sign_flips)
    return (input_grad, weight_grad)


def solution(mesh):
    torus = Mesh(mesh.devices.reshape(NZ, NC, NX, NY), AXES)
    rows = P(AXES, None)
    part = P(("x", "y"), None)
    return jax.shard_map(
        shards,
        mesh=torus,
        in_specs=(rows, rows, part, part, P()),
        out_specs=(rows, part),
        check_vma=False,
    )
```

```python
import jax
import jax.numpy as jnp
import numpy as np
from jax import lax
from jax.experimental import pallas as pl
from jax.experimental.pallas import tpu as pltpu
from jax.sharding import Mesh, PartitionSpec as P

NZ, NC, NX, NY = 8, 2, 4, 4
AXES = ("z", "core", "x", "y")
KV = 1024
TOK = 512
F32, BF16, I16, I32 = jnp.float32, jnp.bfloat16, jnp.int16, jnp.int32
VMEM = 56 * 1024 * 1024
SMALL = 24 * 1024 * 1024


def hadamard(size):
    positions = np.arange(size)
    common = positions[:, None] & positions[None, :]
    parity = np.zeros((size, size), np.int64)
    for bit in range(16):
        parity += (common >> bit) & 1
    return (1 - 2 * (parity & 1)).astype(np.float32)


def power(e):
    return jnp.exp2(e * 0.125)


def step_of(top, low):
    return jnp.ceil(jnp.log2(jnp.maximum(top, low)) * 8.0)


def encode(v, ce):
    u = v if ce is None else v * power(-ce)
    e = step_of(jnp.max(jnp.abs(u), axis=1, keepdims=True), 1e-30) - 119.0
    q = jnp.floor(u * power(-e) + 0.5)
    return q.astype(I32).astype(I16), e


def to_float(q):
    return q.astype(I32).astype(F32)


def eye():
    return lax.broadcasted_iota(I32, (128, 128), 0) == lax.broadcasted_iota(I32, (128, 128), 1)


def to_lanes(col):
    return jnp.sum(jnp.where(eye(), col, 0.0), axis=0, keepdims=True)


def to_rows(row):
    return jnp.sum(jnp.where(eye(), row, 0.0), axis=1, keepdims=True)


def write(msg, v, ce):
    count = v.shape[0]
    q, e = encode(v, ce)
    msg[0:count, :] = q
    parts = [to_lanes(e[k : k + 128]) for k in range(0, count, 128)]
    line = jnp.concatenate(parts + [jnp.zeros((1, KV - count), F32)], 1)
    row = lax.broadcasted_iota(I32, (16, KV), 0)
    extra = jnp.where(row == 0, line, jnp.where(row == 1, ce, 0.0))
    msg[count : count + 16, :] = extra.astype(I32).astype(I16)


def steps_in(msg):
    count = msg.shape[0] - 16
    return to_float(msg[count : count + 16, :])


def read(msg):
    count = msg.shape[0] - 16
    extra = steps_in(msg)
    e = jnp.concatenate([to_rows(extra[0:1, k : k + 128]) for k in range(0, count, 128)], 0)
    return to_float(msg[0:count, :]) * power(e) * power(extra[1:2, :])


def product(tiles, c):
    a = jnp.concatenate([t[...] for t in tiles], 1)
    return lax.dot_general(a, c[...], (((0,), (0,)), ((), ())), preferred_element_type=F32)


def column_steps(c):
    top = jnp.max(jnp.abs(c.astype(F32)), axis=0, keepdims=True)
    return jnp.clip(step_of(top, 1e-30), -800.0, 800.0)


def half(v, number):
    return jnp.concatenate([v[k + 64 * number : k + 64 * number + 64] for k in range(0, v.shape[0], 128)], 0)


def far_kernel(idx, t0, t1, t2, t3, c, *refs):
    up, down, ce = refs[-3:]
    ce[...] = jnp.broadcast_to(column_steps(c[...]), (8, KV))
    p = product((t0, t1, t2, t3), c)
    write(up, half(p, 0), ce[0:1, :])
    write(down, half(p, 1), ce[0:1, :])


def near_kernel(idx, t0, t1, t2, t3, c, ce, up_x, down_x, up_y, down_y, keep):
    p = product((t0, t1, t2, t3), c)
    for step, msg in enumerate((up_x, down_x, up_y, down_y)):

        @pl.when(pl.program_id(0) == step)
        def _(step=step, msg=msg):
            kept = step % 2
            keep[...] = half(p, kept)
            write(msg, half(p, 1 - kept), ce[0:1, :])


def own_kernel(idx, t0, t1, t2, t3, c, keep):
    keep[...] = product((t0, t1, t2, t3), c)


def relay_kernel(keep, ce, *refs):
    for step in range(4):

        @pl.when(pl.program_id(0) == step)
        def _(got=refs[step], msg=refs[4 + step]):
            write(msg, keep[...] + read(got), jnp.maximum(ce[0:1, :], steps_in(got)[1:2, :]))


def cross_kernel(keep, ce, *refs):
    for axis in range(2):

        @pl.when(pl.program_id(0) == axis)
        def _(got=refs[4 * axis : 4 * axis + 4], out=refs[8 + 4 * axis : 12 + 4 * axis]):
            up2, down2, up3, down3 = got
            ce_all = ce[0:1, :]
            for msg in got:
                ce_all = jnp.maximum(ce_all, steps_in(msg)[1:2, :])
            first, last = read(up3) + read(down2), read(up2) + read(down3)
            for t in range(4):
                rows = slice(t * 64, t * 64 + 64)
                total = keep[t * 128 : t * 128 + 128, :] + jnp.concatenate([first[rows], last[rows]], 0)
                if t == 0:
                    out[0][...] = total
                else:
                    write(out[t], total, ce_all)


def split_dot(x, m):
    hi = x.astype(BF16)
    rest = x - hi.astype(F32)
    mid = rest.astype(BF16)
    lo = (rest - mid.astype(F32)).astype(BF16)
    dot = lambda a: jnp.dot(a, m, preferred_element_type=F32)
    return dot(hi) + (dot(mid) + dot(lo))


def split_dot_left(m, x):
    hi = x.astype(BF16)
    rest = x - hi.astype(F32)
    mid = rest.astype(BF16)
    lo = (rest - mid.astype(F32)).astype(BF16)
    dot = lambda a: jnp.dot(m, a, preferred_element_type=F32)
    return dot(hi) + (dot(mid) + dot(lo))


def rotate(v, inner, rows):
    tiles = [v[:, k * 128 : (k + 1) * 128] for k in range(8)]
    for bit in (1, 2, 4):
        tiles = [tiles[k ^ bit] - tiles[k] if k & bit else tiles[k] + tiles[k ^ bit] for k in range(8)]
    mixed = jnp.concatenate([split_dot(t, inner) for t in tiles], 1)
    return split_dot_left(rows, mixed) * (1.0 / 64.0)


def rotate_kernel(own, n1, n2, n3, signs, inner, rows, *refs):
    out = refs[-1]
    total = own[...]
    for msg in (n1, n2, n3):
        total = total + read(msg)
    q, e = encode(rotate(total * signs[...].astype(F32), inner[...], rows[...]), None)
    out[:, 0:KV] = q
    out[:, KV : KV + 128] = jnp.broadcast_to(e, (128, 128)).astype(I32).astype(I16)


def levels_kernel(count, x, inner, rows, after, out):
    level = count[0].astype(F32)

    def group(g):
        q = x[g * 16 : g * 16 + 16, :]
        e = to_float(q[:, KV : KV + 128])[:, 0:1]
        return to_float(q[:, 0:KV]) * power(e)

    groups = [group(g) for g in range(NZ * NC)]
    top = jnp.abs(groups[0])
    for v in groups[1:]:
        top = jnp.maximum(top, jnp.abs(v))
    top = jnp.max(top, axis=1, keepdims=True)
    block = lax.shift_right_logical(lax.broadcasted_iota(I32, (16, 1), 0), 2)
    peak = jnp.zeros((16, 1), F32)
    for b in range(4):
        peak = jnp.where(block == b, jnp.max(jnp.where(block == b, top, 0.0), axis=0, keepdims=True), peak)
    peak = peak + 1e-06
    scale = level / peak
    total = jnp.floor(groups[0] * scale + 0.5)
    for v in groups[1:]:
        total = total + jnp.floor(v * scale + 0.5)
    q, e = encode(rotate(total * (peak / level), inner[...], rows[...]), None)
    out[:, 0:KV] = q
    out[:, KV : KV + 128] = jnp.broadcast_to(e, (16, 128)).astype(I32).astype(I16)


def finish_kernel(q, signs, out):
    e = to_float(q[:, KV : KV + 128])[:, 0:1]
    out[...] = signs[...].astype(F32) * (to_float(q[:, 0:KV]) * power(e))


def input_grad_kernel(at, c, w_own, w_oth, out, w):
    for j in range(2):
        here = ((at[1] + 4 - j - 2 * at[2]) % 4) * 256
        there = ((at[1] + 2 - j + 2 * at[2]) % 4) * 256
        for z in range(NZ):
            w[pl.ds(pl.multiple_of(here + z * 32, 32), 32), :] = w_own[z, j, 0]
            w[pl.ds(pl.multiple_of(there + z * 32, 32), 32), :] = w_oth[z, j, 0]
    out[...] = lax.dot_general(c[...], w[...], (((1,), (1,)), ((), ())), preferred_element_type=F32).astype(BF16)


def tie_kernel(w, after, out):
    del w, after, out


def tie(v, after):
    return pl.pallas_call(
        tie_kernel,
        out_shape=jax.ShapeDtypeStruct(v.shape, v.dtype),
        in_specs=[pl.BlockSpec(memory_space=pl.ANY)] * 2,
        out_specs=pl.BlockSpec(memory_space=pl.ANY),
        input_output_aliases={0: 0},
        name="tie",
    )(v, after)


def params(limit=VMEM):
    return pltpu.CompilerParams(vmem_limit_bytes=limit)


def cost(flops, moved):
    return pl.CostEstimate(flops=int(flops), bytes_accessed=int(moved), transcendentals=0)


def whole(shape):
    return pl.BlockSpec(shape, lambda *_: (0,) * len(shape))


def shift(size, s):
    return [(k, (k + s) % size) for k in range(size)]


def shards(activations, cotangent, value_weights, sign_flips, level_count):
    core = lax.axis_index("core").astype(I32)
    x, y = lax.axis_index("x").astype(I32), lax.axis_index("y").astype(I32)
    sds = jax.ShapeDtypeStruct
    anywhere = pl.BlockSpec(memory_space=pl.ANY)
    in_hbm = lambda v: pltpu.with_memory_space_constraint(v, pltpu.HBM)
    in_vmem = pl.BlockSpec(memory_space=pltpu.VMEM)

    def send(v, axis, s):
        return lax.ppermute(v, "xy"[axis], shift((NX, NY)[axis], s))

    ids = []
    for axis in range(2):
        for dp in range(4):
            for dq in range(4):
                tx = (x + (dq if axis else dp)) % NX
                ty = (y + (dp if axis else dq)) % NY
                ids.append(2 * (tx * NY + ty) + axis)
    idx = jnp.stack(ids).astype(I32)

    z = lax.axis_index("z").astype(I32)

    def along_y(v, steps):
        pairs = []
        for c, step in enumerate(steps):
            if step is not None:
                for k in range(NY):
                    pairs.append((c * NY + k, c * NY + (k + step) % NY))
        return lax.ppermute(v, ("core", "y"), pairs)

    piece = lax.dynamic_slice_in_dim(value_weights, z * 32, 32, 0)
    round1 = [lax.ppermute(piece, "x", shift(NX, s)) for s in (1, 2, 3)]

    def operands(where):
        tiles = [pl.BlockSpec((TOK, 128), lambda k, ids, t=t: (0, ids[where(k) + t])) for t in range(4)]
        return tiles + [whole((TOK, KV))]

    inputs = (in_hbm(activations),) * 4 + (in_hbm(cotangent),)
    message = pltpu.HBM((272, KV), I16)
    mm = 2 * 1024 * 1024 * 512

    def far(axis, *after):
        return pl.pallas_call(
            far_kernel,
            out_shape=(message, message, sds((8, KV), F32)),
            grid_spec=pltpu.PrefetchScalarGridSpec(
                num_scalar_prefetch=1,
                grid=(1,),
                in_specs=operands(lambda k: 16 * axis + 8) + [anywhere] * len(after),
                out_specs=(whole((272, KV)), whole((272, KV)), whole((8, KV))),
            ),
            compiler_params=params(SMALL),
            cost_estimate=cost(mm // 2, 3 << 20),
            name="far",
        )(idx, *inputs, *after)

    up1x, down1x, ce = far(0)
    piece = jnp.concatenate([piece, tie(round1[0], up1x)] + round1[1:], 0)
    came1 = along_y(piece, (1, 2))
    came2 = along_y(piece, (None, 3))
    up1y, down1y, _ = far(1, piece)
    came1 = tie(came1, up1y)
    piece = jnp.concatenate([jnp.where(core == 0, piece, came1), jnp.where(core == 0, came1, came2)], 0)
    w_own = lax.all_gather(piece, "z", axis=0, tiled=True)
    got1 = [send(up1x, 0, 1), send(down1x, 0, -1), send(up1y, 1, 1), send(down1y, 1, -1)]

    up2x, down2x, up2y, down2y, keep_near = pl.pallas_call(
        near_kernel,
        out_shape=(message,) * 4 + (sds((1024, KV), F32),),
        grid_spec=pltpu.PrefetchScalarGridSpec(
            num_scalar_prefetch=1,
            grid=(4,),
            in_specs=operands(lambda k: 16 * (k // 2) + 4 + 8 * (k % 2)) + [whole((8, KV))],
            out_specs=(whole((272, KV)),) * 4 + (pl.BlockSpec((256, KV), lambda k, ids: (k, 0)),),
        ),
        compiler_params=params(SMALL),
        cost_estimate=cost(2 * mm, 11 << 20),
        name="near",
    )(idx, *inputs, ce)
    got2 = [send(up2x, 0, 1), send(down2x, 0, -1), send(up2y, 1, 1), send(down2y, 1, -1)]

    keep = pl.pallas_call(
        own_kernel,
        out_shape=sds((1024, KV), F32),
        grid_spec=pltpu.PrefetchScalarGridSpec(
            num_scalar_prefetch=1,
            grid=(2,),
            in_specs=operands(lambda k: 16 * k),
            out_specs=pl.BlockSpec((512, KV), lambda k, ids: (k, 0)),
        ),
        compiler_params=params(SMALL),
        cost_estimate=cost(mm, 8 << 20),
        name="own",
    )(idx, *inputs)

    up3x, down3x, up3y, down3y = pl.pallas_call(
        relay_kernel,
        out_shape=(message,) * 4,
        grid=(4,),
        in_specs=[pl.BlockSpec((256, KV), lambda k: (k, 0)), whole((8, KV))] + [whole((272, KV))] * 4,
        out_specs=(whole((272, KV)),) * 4,
        compiler_params=params(SMALL),
        cost_estimate=cost(1 << 20, 8 << 20),
        name="relay",
    )(keep_near, ce, *got1)
    got3 = [send(up3x, 0, 1), send(down3x, 0, -1), send(up3y, 1, 1), send(down3y, 1, -1)]

    parts = pl.pallas_call(
        cross_kernel,
        out_shape=((pltpu.HBM((128, KV), F32),) + (pltpu.HBM((144, KV), I16),) * 3) * 2,
        grid=(2,),
        in_specs=[pl.BlockSpec((512, KV), lambda k: (k, 0)), whole((8, KV))] + [whole((272, KV))] * 8,
        out_specs=((whole((128, KV)),) + (whole((144, KV)),) * 3) * 2,
        compiler_params=params(SMALL),
        cost_estimate=cost(1 << 20, 12 << 20),
        name="cross",
    )(keep, ce, got2[0], got2[1], got3[0], got3[1], got2[2], got2[3], got3[2], got3[3])
    own_x, x1, x2, x3, own_y, y1, y2, y3 = parts
    last = [send(x1, 1, 1), send(x2, 1, 2), send(x3, 1, -1), send(y1, 0, 1), send(y2, 0, 2), send(y3, 0, -1)]

    inner = jnp.asarray(hadamard(128), BF16)
    quad = hadamard(4)
    eights = jnp.asarray(np.kron(np.eye(32), quad), BF16)

    def rotated(axis, own, msgs, *before):
        return pl.pallas_call(
            rotate_kernel,
            out_shape=pltpu.HBM((256, KV + 128), I16),
            grid=(1,),
            in_specs=[whole((128, KV))]
            + [whole((144, KV))] * 3
            + [pl.BlockSpec((128, KV), lambda k: (axis, 0)), whole((128, 128)), whole((128, 128))]
            + [anywhere] * len(before),
            out_specs=pl.BlockSpec((128, KV + 128), lambda k: (axis, 0)),
            input_output_aliases={7: 0} if before else {},
            compiler_params=params(SMALL),
            cost_estimate=cost(1 << 27, 2 << 20),
            name="rotate",
        )(in_hbm(own), *msgs, sign_flips, inner, eights, *before)

    spun = rotated(1, own_y, last[3:], rotated(0, own_x, last[:3]))
    groups = lax.all_to_all(spun, ("z", "core"), 0, 0, tiled=True)

    w_own = tie(w_own, spun)
    w_oth = lax.ppermute(w_own, "core", shift(NC, 1))
    place = jnp.stack([x, y, core]).astype(I32)
    w_block = pl.BlockSpec((NZ, 2, 1, 32, KV), lambda k, at: (0, 0, k, 0, 0))
    input_grad = pl.pallas_call(
        input_grad_kernel,
        out_shape=pltpu.HBM((TOK, 4096), BF16),
        grid_spec=pltpu.PrefetchScalarGridSpec(
            num_scalar_prefetch=1,
            grid=(4,),
            in_specs=[whole((TOK, KV)), w_block, w_block],
            out_specs=pl.BlockSpec((TOK, 1024), lambda k, at: (0, (at[0] + 4 - k) % 4)),
            scratch_shapes=[pltpu.VMEM((1024, KV), BF16)],
        ),
        compiler_params=params(SMALL),
        cost_estimate=cost(4 * mm, 13 << 20),
        name="input_grad",
    )(place, cotangent, w_own.reshape(NZ, 2, 4, 32, KV), w_oth.reshape(NZ, 2, 4, 32, KV))

    back = pl.pallas_call(
        levels_kernel,
        out_shape=sds((16, KV + 128), I16),
        in_specs=[pl.BlockSpec(memory_space=pltpu.SMEM)] + [in_vmem] * 3 + [anywhere],
        out_specs=in_vmem,
        compiler_params=params(SMALL),
        cost_estimate=cost(1 << 26, 1 << 20),
        name="levels",
    )(level_count.reshape(1), groups, inner, jnp.asarray(np.kron(np.eye(4), quad), BF16), in_hbm(input_grad))
    gathered = lax.all_gather(back, ("z", "core"), axis=0, tiled=True)
    weight_grad = pl.pallas_call(
        finish_kernel,
        out_shape=sds((256, KV), F32),
        in_specs=[in_vmem] * 2,
        out_specs=in_vmem,
        compiler_params=params(SMALL),
        cost_estimate=cost(1 << 20, 3 << 20),
        name="finish",
    )(gathered, sign_flips)
    return (input_grad, weight_grad)


def solution(mesh):
    torus = Mesh(mesh.devices.reshape(NZ, NC, NX, NY), AXES)
    rows = P(AXES, None)
    part = P(("x", "y"), None)
    return jax.shard_map(
        shards,
        mesh=torus,
        in_specs=(rows, rows, part, part, P()),
        out_specs=(rows, part),
        check_vma=False,
    )
```

```python
import jax
import jax.numpy as jnp
import numpy as np
from jax import lax
from jax.experimental import pallas as pl
from jax.experimental.pallas import tpu as pltpu
from jax.sharding import Mesh, PartitionSpec as P

NZ, NC, NX, NY = 8, 2, 4, 4
AXES = ("z", "core", "x", "y")
KV = 1024
TOK = 512
F32, BF16, I16, I32 = jnp.float32, jnp.bfloat16, jnp.int16, jnp.int32
VMEM = 56 * 1024 * 1024
SMALL = 24 * 1024 * 1024


def hadamard(size):
    positions = np.arange(size)
    common = positions[:, None] & positions[None, :]
    parity = np.zeros((size, size), np.int64)
    for bit in range(16):
        parity += (common >> bit) & 1
    return (1 - 2 * (parity & 1)).astype(np.float32)


def power(e):
    return jnp.exp2(e * 0.125)


def step_of(top, low):
    return jnp.ceil(jnp.log2(jnp.maximum(top, low)) * 8.0)


def encode(v, ce):
    u = v if ce is None else v * power(-ce)
    e = step_of(jnp.max(jnp.abs(u), axis=1, keepdims=True), 1e-30) - 119.0
    q = jnp.floor(u * power(-e) + 0.5)
    return q.astype(I32).astype(I16), e


def to_float(q):
    return q.astype(I32).astype(F32)


def eye():
    return lax.broadcasted_iota(I32, (128, 128), 0) == lax.broadcasted_iota(I32, (128, 128), 1)


def to_lanes(col):
    return jnp.sum(jnp.where(eye(), col, 0.0), axis=0, keepdims=True)


def to_rows(row):
    return jnp.sum(jnp.where(eye(), row, 0.0), axis=1, keepdims=True)


def write(msg, v, ce):
    count = v.shape[0]
    q, e = encode(v, ce)
    msg[0:count, :] = q
    parts = [to_lanes(e[k : k + 128]) for k in range(0, count, 128)]
    line = jnp.concatenate(parts + [jnp.zeros((1, KV - count), F32)], 1)
    row = lax.broadcasted_iota(I32, (16, KV), 0)
    extra = jnp.where(row == 0, line, jnp.where(row == 1, ce, 0.0))
    msg[count : count + 16, :] = extra.astype(I32).astype(I16)


def steps_in(msg):
    count = msg.shape[0] - 16
    return to_float(msg[count : count + 16, :])


def read(msg):
    count = msg.shape[0] - 16
    extra = steps_in(msg)
    e = jnp.concatenate([to_rows(extra[0:1, k : k + 128]) for k in range(0, count, 128)], 0)
    return to_float(msg[0:count, :]) * power(e) * power(extra[1:2, :])


def product(tiles, c):
    a = jnp.concatenate([t[...] for t in tiles], 1)
    return lax.dot_general(a, c[...], (((0,), (0,)), ((), ())), preferred_element_type=F32)


def column_steps(c):
    top = jnp.max(jnp.abs(c.astype(F32)), axis=0, keepdims=True)
    return jnp.clip(step_of(top, 1e-30), -800.0, 800.0)


def half(v, number):
    return jnp.concatenate([v[k + 64 * number : k + 64 * number + 64] for k in range(0, v.shape[0], 128)], 0)


def far_kernel(idx, t0, t1, t2, t3, c, *refs):
    up, down, ce = refs[-3:]
    ce[...] = jnp.broadcast_to(column_steps(c[...]), (8, KV))
    p = product((t0, t1, t2, t3), c)
    write(up, half(p, 0), ce[0:1, :])
    write(down, half(p, 1), ce[0:1, :])


def near_kernel(idx, t0, t1, t2, t3, c, ce, up_x, down_x, up_y, down_y, keep):
    p = product((t0, t1, t2, t3), c)
    for step, msg in enumerate((up_x, down_x, up_y, down_y)):

        @pl.when(pl.program_id(0) == step)
        def _(step=step, msg=msg):
            kept = step % 2
            keep[...] = half(p, kept)
            write(msg, half(p, 1 - kept), ce[0:1, :])


def own_kernel(idx, t0, t1, t2, t3, c, keep):
    keep[...] = product((t0, t1, t2, t3), c)


def relay_kernel(keep, ce, *refs):
    for step in range(4):

        @pl.when(pl.program_id(0) == step)
        def _(got=refs[step], msg=refs[4 + step]):
            write(msg, keep[...] + read(got), jnp.maximum(ce[0:1, :], steps_in(got)[1:2, :]))


def cross_kernel(keep, ce, *refs):
    for axis in range(2):

        @pl.when(pl.program_id(0) == axis)
        def _(got=refs[4 * axis : 4 * axis + 4], out=refs[8 + 4 * axis : 12 + 4 * axis]):
            up2, down2, up3, down3 = got
            ce_all = ce[0:1, :]
            for msg in got:
                ce_all = jnp.maximum(ce_all, steps_in(msg)[1:2, :])
            first, last = read(up3) + read(down2), read(up2) + read(down3)
            for t in range(4):
                rows = slice(t * 64, t * 64 + 64)
                total = keep[t * 128 : t * 128 + 128, :] + jnp.concatenate([first[rows], last[rows]], 0)
                if t == 0:
                    out[0][...] = total
                else:
                    write(out[t], total, ce_all)


def split_dot(x, m):
    hi = x.astype(BF16)
    rest = x - hi.astype(F32)
    mid = rest.astype(BF16)
    lo = (rest - mid.astype(F32)).astype(BF16)
    dot = lambda a: jnp.dot(a, m, preferred_element_type=F32)
    return dot(hi) + (dot(mid) + dot(lo))


def split_dot_left(m, x):
    hi = x.astype(BF16)
    rest = x - hi.astype(F32)
    mid = rest.astype(BF16)
    lo = (rest - mid.astype(F32)).astype(BF16)
    dot = lambda a: jnp.dot(m, a, preferred_element_type=F32)
    return dot(hi) + (dot(mid) + dot(lo))


def rotate(v, inner, rows):
    tiles = [v[:, k * 128 : (k + 1) * 128] for k in range(8)]
    for bit in (1, 2, 4):
        tiles = [tiles[k ^ bit] - tiles[k] if k & bit else tiles[k] + tiles[k ^ bit] for k in range(8)]
    mixed = jnp.concatenate([split_dot(t, inner) for t in tiles], 1)
    return split_dot_left(rows, mixed) * (1.0 / 64.0)


def rotate_kernel(own, n1, n2, n3, signs, inner, rows, *refs):
    out = refs[-1]
    total = own[...]
    for msg in (n1, n2, n3):
        total = total + read(msg)
    q, e = encode(rotate(total * signs[...].astype(F32), inner[...], rows[...]), None)
    out[:, 0:KV] = q
    out[:, KV : KV + 128] = jnp.broadcast_to(e, (128, 128)).astype(I32).astype(I16)


def levels_kernel(count, x, inner, rows, after, out):
    level = count[0].astype(F32)

    def group(g):
        q = x[g * 16 : g * 16 + 16, :]
        e = to_float(q[:, KV : KV + 128])[:, 0:1]
        return to_float(q[:, 0:KV]) * power(e)

    groups = [group(g) for g in range(NZ * NC)]
    top = jnp.abs(groups[0])
    for v in groups[1:]:
        top = jnp.maximum(top, jnp.abs(v))
    top = jnp.max(top, axis=1, keepdims=True)
    block = lax.shift_right_logical(lax.broadcasted_iota(I32, (16, 1), 0), 2)
    peak = jnp.zeros((16, 1), F32)
    for b in range(4):
        peak = jnp.where(block == b, jnp.max(jnp.where(block == b, top, 0.0), axis=0, keepdims=True), peak)
    peak = peak + 1e-06
    scale = level / peak
    total = jnp.floor(groups[0] * scale + 0.5)
    for v in groups[1:]:
        total = total + jnp.floor(v * scale + 0.5)
    q, e = encode(rotate(total * (peak / level), inner[...], rows[...]), None)
    out[:, 0:KV] = q
    out[:, KV : KV + 128] = jnp.broadcast_to(e, (16, 128)).astype(I32).astype(I16)


def finish_kernel(q, signs, out):
    e = to_float(q[:, KV : KV + 128])[:, 0:1]
    out[...] = signs[...].astype(F32) * (to_float(q[:, 0:KV]) * power(e))


def input_grad_kernel(at, c, w_own, w_oth, out, w):
    for j in range(4):
        chip = ((at[1] + 4 - j) % 4) * 256
        for z in range(NZ):
            w[pl.ds(pl.multiple_of(chip + z * 32 + at[2] * 16, 16), 16), :] = w_own[z, j, 0]
            w[pl.ds(pl.multiple_of(chip + z * 32 + 16 - at[2] * 16, 16), 16), :] = w_oth[z, j, 0]
    out[...] = lax.dot_general(c[...], w[...], (((1,), (1,)), ((), ())), preferred_element_type=F32).astype(BF16)


def tie_kernel(w, after, out):
    del w, after, out


def tie(v, after):
    return pl.pallas_call(
        tie_kernel,
        out_shape=jax.ShapeDtypeStruct(v.shape, v.dtype),
        in_specs=[pl.BlockSpec(memory_space=pl.ANY)] * 2,
        out_specs=pl.BlockSpec(memory_space=pl.ANY),
        input_output_aliases={0: 0},
        name="tie",
    )(v, after)


def params(limit=VMEM):
    return pltpu.CompilerParams(vmem_limit_bytes=limit)


def cost(flops, moved):
    return pl.CostEstimate(flops=int(flops), bytes_accessed=int(moved), transcendentals=0)


def whole(shape):
    return pl.BlockSpec(shape, lambda *_: (0,) * len(shape))


def shift(size, s):
    return [(k, (k + s) % size) for k in range(size)]


def shards(activations, cotangent, value_weights, sign_flips, level_count):
    core = lax.axis_index("core").astype(I32)
    x, y = lax.axis_index("x").astype(I32), lax.axis_index("y").astype(I32)
    sds = jax.ShapeDtypeStruct
    anywhere = pl.BlockSpec(memory_space=pl.ANY)
    in_hbm = lambda v: pltpu.with_memory_space_constraint(v, pltpu.HBM)
    in_vmem = pl.BlockSpec(memory_space=pltpu.VMEM)

    def send(v, axis, s):
        return lax.ppermute(v, "xy"[axis], shift((NX, NY)[axis], s))

    ids = []
    for axis in range(2):
        for dp in range(4):
            for dq in range(4):
                tx = (x + (dq if axis else dp)) % NX
                ty = (y + (dp if axis else dq)) % NY
                ids.append(2 * (tx * NY + ty) + axis)
    idx = jnp.stack(ids).astype(I32)

    z = lax.axis_index("z").astype(I32)

    def spread(piece, axis):
        return [lax.ppermute(piece, axis, shift(4, s)) for s in (1, 2, 3)]

    piece = lax.dynamic_slice_in_dim(value_weights, (2 * z + core) * 16, 16, 0)
    round1 = spread(piece, "x")

    def operands(where):
        tiles = [pl.BlockSpec((TOK, 128), lambda k, ids, t=t: (0, ids[where(k) + t])) for t in range(4)]
        return tiles + [whole((TOK, KV))]

    inputs = (in_hbm(activations),) * 4 + (in_hbm(cotangent),)
    message = pltpu.HBM((272, KV), I16)
    mm = 2 * 1024 * 1024 * 512

    def far(axis, *after):
        return pl.pallas_call(
            far_kernel,
            out_shape=(message, message, sds((8, KV), F32)),
            grid_spec=pltpu.PrefetchScalarGridSpec(
                num_scalar_prefetch=1,
                grid=(1,),
                in_specs=operands(lambda k: 16 * axis + 8) + [anywhere] * len(after),
                out_specs=(whole((272, KV)), whole((272, KV)), whole((8, KV))),
            ),
            compiler_params=params(SMALL),
            cost_estimate=cost(mm // 2, 3 << 20),
            name="far",
        )(idx, *inputs, *after)

    up1x, down1x, ce = far(0)
    piece = jnp.concatenate([piece, tie(round1[0], up1x)] + round1[1:], 0)
    round2 = spread(piece, "y")
    up1y, down1y, _ = far(1, piece)
    piece = jnp.concatenate([piece, tie(round2[0], up1y)] + round2[1:], 0)
    w_own = lax.all_gather(piece, "z", axis=0, tiled=True)
    got1 = [send(up1x, 0, 1), send(down1x, 0, -1), send(up1y, 1, 1), send(down1y, 1, -1)]

    up2x, down2x, up2y, down2y, keep_near = pl.pallas_call(
        near_kernel,
        out_shape=(message,) * 4 + (sds((1024, KV), F32),),
        grid_spec=pltpu.PrefetchScalarGridSpec(
            num_scalar_prefetch=1,
            grid=(4,),
            in_specs=operands(lambda k: 16 * (k // 2) + 4 + 8 * (k % 2)) + [whole((8, KV))],
            out_specs=(whole((272, KV)),) * 4 + (pl.BlockSpec((256, KV), lambda k, ids: (k, 0)),),
        ),
        compiler_params=params(SMALL),
        cost_estimate=cost(2 * mm, 11 << 20),
        name="near",
    )(idx, *inputs, ce)
    got2 = [send(up2x, 0, 1), send(down2x, 0, -1), send(up2y, 1, 1), send(down2y, 1, -1)]

    keep = pl.pallas_call(
        own_kernel,
        out_shape=sds((1024, KV), F32),
        grid_spec=pltpu.PrefetchScalarGridSpec(
            num_scalar_prefetch=1,
            grid=(2,),
            in_specs=operands(lambda k: 16 * k),
            out_specs=pl.BlockSpec((512, KV), lambda k, ids: (k, 0)),
        ),
        compiler_params=params(SMALL),
        cost_estimate=cost(mm, 8 << 20),
        name="own",
    )(idx, *inputs)

    up3x, down3x, up3y, down3y = pl.pallas_call(
        relay_kernel,
        out_shape=(message,) * 4,
        grid=(4,),
        in_specs=[pl.BlockSpec((256, KV), lambda k: (k, 0)), whole((8, KV))] + [whole((272, KV))] * 4,
        out_specs=(whole((272, KV)),) * 4,
        compiler_params=params(SMALL),
        cost_estimate=cost(1 << 20, 8 << 20),
        name="relay",
    )(keep_near, ce, *got1)
    got3 = [send(up3x, 0, 1), send(down3x, 0, -1), send(up3y, 1, 1), send(down3y, 1, -1)]

    parts = pl.pallas_call(
        cross_kernel,
        out_shape=((pltpu.HBM((128, KV), F32),) + (pltpu.HBM((144, KV), I16),) * 3) * 2,
        grid=(2,),
        in_specs=[pl.BlockSpec((512, KV), lambda k: (k, 0)), whole((8, KV))] + [whole((272, KV))] * 8,
        out_specs=((whole((128, KV)),) + (whole((144, KV)),) * 3) * 2,
        compiler_params=params(SMALL),
        cost_estimate=cost(1 << 20, 12 << 20),
        name="cross",
    )(keep, ce, got2[0], got2[1], got3[0], got3[1], got2[2], got2[3], got3[2], got3[3])
    own_x, x1, x2, x3, own_y, y1, y2, y3 = parts
    last = [send(x1, 1, 1), send(x2, 1, 2), send(x3, 1, -1), send(y1, 0, 1), send(y2, 0, 2), send(y3, 0, -1)]

    inner = jnp.asarray(hadamard(128), BF16)
    quad = hadamard(4)
    eights = jnp.asarray(np.kron(np.eye(32), quad), BF16)

    def rotated(axis, own, msgs, *before):
        return pl.pallas_call(
            rotate_kernel,
            out_shape=pltpu.HBM((256, KV + 128), I16),
            grid=(1,),
            in_specs=[whole((128, KV))]
            + [whole((144, KV))] * 3
            + [pl.BlockSpec((128, KV), lambda k: (axis, 0)), whole((128, 128)), whole((128, 128))]
            + [anywhere] * len(before),
            out_specs=pl.BlockSpec((128, KV + 128), lambda k: (axis, 0)),
            input_output_aliases={7: 0} if before else {},
            compiler_params=params(SMALL),
            cost_estimate=cost(1 << 27, 2 << 20),
            name="rotate",
        )(in_hbm(own), *msgs, sign_flips, inner, eights, *before)

    spun = rotated(1, own_y, last[3:], rotated(0, own_x, last[:3]))
    groups = lax.all_to_all(spun, ("z", "core"), 0, 0, tiled=True)

    w_own = tie(w_own, spun)
    w_oth = lax.ppermute(w_own, "core", shift(NC, 1))
    place = jnp.stack([x, y, core]).astype(I32)
    w_block = pl.BlockSpec((NZ, 4, 1, 16, KV), lambda k, at: (0, 0, k, 0, 0))
    input_grad = pl.pallas_call(
        input_grad_kernel,
        out_shape=pltpu.HBM((TOK, 4096), BF16),
        grid_spec=pltpu.PrefetchScalarGridSpec(
            num_scalar_prefetch=1,
            grid=(4,),
            in_specs=[whole((TOK, KV)), w_block, w_block],
            out_specs=pl.BlockSpec((TOK, 1024), lambda k, at: (0, (at[0] + 4 - k) % 4)),
            scratch_shapes=[pltpu.VMEM((1024, KV), BF16)],
        ),
        compiler_params=params(SMALL),
        cost_estimate=cost(4 * mm, 13 << 20),
        name="input_grad",
    )(place, cotangent, in_hbm(w_own.reshape(NZ, 4, 4, 16, KV)), in_hbm(w_oth.reshape(NZ, 4, 4, 16, KV)))

    back = pl.pallas_call(
        levels_kernel,
        out_shape=sds((16, KV + 128), I16),
        in_specs=[pl.BlockSpec(memory_space=pltpu.SMEM)] + [in_vmem] * 3 + [anywhere],
        out_specs=in_vmem,
        compiler_params=params(SMALL),
        cost_estimate=cost(1 << 26, 1 << 20),
        name="levels",
    )(level_count.reshape(1), groups, inner, jnp.asarray(np.kron(np.eye(4), quad), BF16), in_hbm(input_grad))
    gathered = lax.all_gather(back, ("z", "core"), axis=0, tiled=True)
    weight_grad = pl.pallas_call(
        finish_kernel,
        out_shape=sds((256, KV), F32),
        in_specs=[in_vmem] * 2,
        out_specs=in_vmem,
        compiler_params=params(SMALL),
        cost_estimate=cost(1 << 20, 3 << 20),
        name="finish",
    )(gathered, sign_flips)
    return (input_grad, weight_grad)


def solution(mesh):
    torus = Mesh(mesh.devices.reshape(NZ, NC, NX, NY), AXES)
    rows = P(AXES, None)
    part = P(("x", "y"), None)
    return jax.shard_map(
        shards,
        mesh=torus,
        in_specs=(rows, rows, part, part, P()),
        out_specs=(rows, part),
        check_vma=False,
    )
```
